256 devices in a mesh: row: 16 (over z, y_lo), col: 16 (over y_hi, x, core).
Axes of the slice: x: 4, y: 4 (y_hi: 2, y_lo: 2; y = y_hi * 2 + y_lo), z: 8, core: 2. Of those that a mesh axis runs over, the one named last changes fastest.
Arguments:
- features: float32 [32, 24576], P(None, ('row', 'col')), may hold values from -6 to 6
- block: float32 [16, 24576], P(None, ('row', 'col')), may hold values from -6 to 6
Outputs:
- applied: float32 [16, 24576], P(None, ('row', 'col'))
The draws below stay inside these ranges and needn't reach their ends.
All inputs are finite; a program needn't handle non-finite values.
Results may differ from the reference program's by a relative error of at most 0.006.
Values may be sent and summed in bfloat16 or wider, within the bound.
No kernel may reach another device: no remote copies, remote signals or barrier semaphores. Data moves between devices by JAX's collectives and lax.ppermute only.
A program may use at most 64 MiB of HBM per device.

```python
import math
import jax
import jax.numpy as jnp
from jax import lax

F = 32
BLOCK = 16
FRAMES = 24576


def level_of(own_key, dims, cuts, smallest, high):
    loudness, own = 1.0, jax.random.fold_in(own_key, 6)
    for dim, blocks in cuts:
        draws = jnp.exp(jax.random.uniform(jax.random.fold_in(own, dim), (blocks,), jnp.float32, smallest / len(cuts), high / len(cuts)))
        loudness = loudness * jnp.repeat(draws, dims[dim] // blocks).reshape([-1 if axis == dim else 1 for axis in range(len(dims))])
    return loudness


def normal_values(stream_key, extent, deviation, reach, cuts=(), kind=jnp.bfloat16):
    result = deviation * jax.random.normal(stream_key, extent, jnp.float32)
    if cuts:
        result = result * level_of(stream_key, extent, cuts, -0.22, 0.18)
    return jnp.clip(result, -reach, reach).astype(kind)


def setup_inputs(seed: int = 0) -> dict:
    seeds = jax.random.split(jax.random.key(seed), 3)
    return {
        "features": normal_values(seeds[0], (F, FRAMES), 1.0, 6.0, ((1, 256),), jnp.float32),
        "block": normal_values(seeds[1], (BLOCK, FRAMES), 1.0, 6.0, ((1, 256),), jnp.float32),
    }


def kernel_rows(row_feat, row_sq, col_feat, col_sq, scale, start, count):
    part = lax.dynamic_slice_in_dim(row_feat, start, count, 1)
    sq_part = lax.dynamic_slice_in_dim(row_sq, start, count, 0)
    inner = jnp.einsum('fi,fj->ij', part, col_feat, precision=lax.Precision.HIGHEST)
    dist = sq_part[:, None] + col_sq[None, :] - 2.0 * inner
    return jnp.exp(-dist / scale).astype(jnp.bfloat16)

def reference(features, block):
    scale = 4.0 / (float(FRAMES) ** (2.0 / F) - 1.0)
    sq = lax.optimization_barrier(jnp.sum(features * features, axis=0))
    step = math.gcd(512, FRAMES)
    starts = jnp.arange(FRAMES // step, dtype=jnp.int32) * step

    def tile(start):
        return kernel_rows(features, sq, features, sq, scale, start, step)
    q = lax.map(lambda s: lax.optimization_barrier(jnp.sum(tile(s), axis=1, dtype=jnp.float32)), starts).reshape(-1)
    inv_q = 1.0 / q
    second = lax.map(lambda s: lax.optimization_barrier(jnp.sum(tile(s).astype(jnp.float32) * inv_q[None, :], axis=1)), starts).reshape(-1)
    dens = second * inv_q
    factor = inv_q * lax.rsqrt(dens)
    weighted = (block * factor[None, :]).astype(jnp.bfloat16)
    parts = lax.map(lambda s: jnp.dot(tile(s), weighted.T, preferred_element_type=jnp.float32), starts)
    summed = parts.reshape(FRAMES, BLOCK).T
    return summed * factor[None, :]
```

```python
import functools
import math

import jax
import jax.numpy as jnp
from jax import lax
from jax.experimental import pallas as pl
from jax.experimental.pallas import tpu as pltpu
from jax.sharding import Mesh, PartitionSpec as P

f32 = jnp.float32
bf16 = jnp.bfloat16
VMEM = pl.BlockSpec(memory_space=pltpu.VMEM)
PARAMS = pltpu.CompilerParams(vmem_limit_bytes=40 * 1024 * 1024)

GROUP_X = "col"
GROUP_Y = "row"


def three_parts(v):
    high = v.astype(bf16)
    rest = v - high.astype(f32)
    mid = rest.astype(bf16)
    low = (rest - mid.astype(f32)).astype(bf16)
    return high, mid, low


def extended(v, left):
    high, mid, low = three_parts(v)
    half = -0.5 * jnp.sum(v * v, axis=0, keepdims=True)
    a, b, c = (p.astype(f32) for p in three_parts(half))
    row = lax.broadcasted_iota(jnp.int32, (16, v.shape[1]), 0)
    base = 0 if left else 3
    ones = jnp.where((row >= 3 - base) & (row < 6 - base), 1.0, 0.0)
    tail = jnp.where(row == base, a, jnp.where(row == base + 1, b, jnp.where(row == base + 2, c, ones)))
    tail = tail.astype(bf16)
    if left:
        parts = [high, high, mid, high, low, mid, tail]
    else:
        parts = [high, mid, high, low, high, mid, tail]
    return jnp.concatenate(parts, axis=0)


def kernel_block(gain, x_ref, y_ref, k_ref, q_ref, col_ref, right_ref):
    count, _, width = x_ref.shape
    total = k_ref.shape[1]
    y = jnp.concatenate([y_ref[i] for i in range(count)], axis=1) * gain
    right_ref[...] = extended(y, False)
    step = 512
    col_ref[...] = jnp.zeros_like(col_ref)
    for i in range(count):
        left = extended(x_ref[i] * gain, True)
        lanes = jnp.zeros((width, 128), f32)
        for j in range(0, total, step):
            expo = lax.dot_general(
                left, right_ref[:, j : j + step], (((0,), (0,)), ((), ())),
                preferred_element_type=f32,
            )
            tile = jnp.exp2(expo).astype(bf16)
            k_ref[i * width : (i + 1) * width, j : j + step] = tile
            wide = tile.astype(f32)
            col_ref[:, j : j + step] += jnp.sum(wide, axis=0, keepdims=True)
            for t in range(0, step, 128):
                lanes = lanes + wide[:, t : t + 128]
        sums = jnp.sum(lanes.T, axis=0, keepdims=True)
        for d in range(count):
            q_ref[d, i : i + 1, :] = sums


def second_block(q_ref, k_ref, col_ref, out_ref):
    count, _, width = q_ref.shape
    total = k_ref.shape[1]
    inv = 1.0 / jnp.sum(q_ref[...], axis=0)
    acc = jnp.zeros((8, total), f32)
    for i in range(count):
        tall = jnp.broadcast_to(inv[i : i + 1, :], (128, width)).T
        for r in range(0, width, 16):
            rows = k_ref[i * width + r : i * width + r + 16, :].astype(f32)
            w = tall[r : r + 16, :]
            prod = jnp.concatenate(
                [rows[:, t : t + 128] * w for t in range(0, total, 128)], axis=1
            )
            acc = acc + prod[:8] + prod[8:]
    second = jnp.sum(acc, axis=0, keepdims=True)
    for d in range(count):
        out_ref[d, 0:1, :] = col_ref[...]
        out_ref[d, 1:2, :] = second


def product_block(m_ref, k_ref, b_ref, out_ref, fac_ref):
    count, _, width = b_ref.shape
    sums = jnp.sum(m_ref[...], axis=0)
    inv = 1.0 / sums[0:1]
    factor = inv * lax.rsqrt(sums[1:2] * inv)
    block = jnp.concatenate([b_ref[i] for i in range(count)], axis=1)
    weighted = (block * factor).astype(bf16)
    for i in range(count):
        out_ref[i] = lax.dot_general(
            weighted, k_ref[i * width : (i + 1) * width, :], (((1,), (1,)), ((), ())),
            preferred_element_type=f32,
        )
        fac_ref[i] = factor[:, i * width : (i + 1) * width]


def per_device(features, block):
    width, owned = features.shape
    n = lax.axis_size(GROUP_X)
    m = lax.axis_size(GROUP_Y)
    frames = owned * n * m
    scale = 4.0 / (float(frames) ** (2.0 / width) - 1.0)
    gain = math.sqrt(2.0 * math.log2(math.e) / scale)
    k_rows, k_cols = n * owned, m * owned

    def to_all(x, axis):
        copies = jnp.broadcast_to(x, (lax.axis_size(axis), *x.shape))
        return lax.all_to_all(copies, axis, 0, 0, tiled=True)

    x_feat = lax.all_gather(features, GROUP_X)
    y_block = lax.all_gather(block, GROUP_Y)
    y_feat = to_all(features, GROUP_Y)
    kern, q_parts, col_sum = pl.pallas_call(
        functools.partial(kernel_block, gain),
        out_shape=(
            jax.ShapeDtypeStruct((k_rows, k_cols), bf16),
            jax.ShapeDtypeStruct((n, n, owned), f32),
            jax.ShapeDtypeStruct((1, k_cols), f32),
        ),
        in_specs=[VMEM] * 2,
        out_specs=(VMEM,) * 3,
        scratch_shapes=[pltpu.VMEM((6 * width + 16, k_cols), bf16)],
        compiler_params=PARAMS,
        name="kernel_block",
    )(x_feat, y_feat)
    q_parts = lax.all_to_all(q_parts, GROUP_X, 0, 0, tiled=True)
    sums = pl.pallas_call(
        second_block,
        out_shape=jax.ShapeDtypeStruct((m, 2, k_cols), f32),
        in_specs=[VMEM] * 3,
        out_specs=VMEM,
        compiler_params=PARAMS,
        name="second_block",
    )(q_parts, kern, col_sum)
    sums = lax.all_to_all(sums, GROUP_Y, 0, 0, tiled=True)
    parts, factor = pl.pallas_call(
        product_block,
        out_shape=(
            jax.ShapeDtypeStruct((n, block.shape[0], owned), f32),
            jax.ShapeDtypeStruct((m, 1, owned), f32),
        ),
        in_specs=[VMEM] * 3,
        out_specs=(VMEM,) * 2,
        compiler_params=PARAMS,
        name="product_block",
    )(sums, kern, y_block)
    parts = lax.all_to_all(parts, GROUP_X, 0, 0, tiled=True)
    own = lax.dynamic_index_in_dim(factor, lax.axis_index(GROUP_Y), 0, keepdims=False)
    return jnp.sum(parts, axis=0) * own


def solution(mesh):
    placed = (P(None, ("row", "col")), P(None, ("row", "col")))
    return jax.shard_map(
        per_device, mesh=mesh, in_specs=placed, out_specs=P(None, ("row", "col")), check_vma=False
    )
```

```python
import functools
import math

import jax
import jax.numpy as jnp
from jax import lax
from jax.experimental import pallas as pl
from jax.experimental.pallas import tpu as pltpu
from jax.sharding import Mesh, PartitionSpec as P

f32 = jnp.float32
bf16 = jnp.bfloat16
VMEM = pl.BlockSpec(memory_space=pltpu.VMEM)
PARAMS = pltpu.CompilerParams(vmem_limit_bytes=16 * 1024 * 1024)

ALL = ("z", "ylo", "yhi", "x", "core")
GROUP_X = ("ylo", "yhi", "x")
GROUP_Y = ("z", "core")


def three_parts(v):
    high = v.astype(bf16)
    rest = v - high.astype(f32)
    mid = rest.astype(bf16)
    low = (rest - mid.astype(f32)).astype(bf16)
    return high, mid, low


def extended(v, left):
    high, mid, low = three_parts(v)
    half = -0.5 * jnp.sum(v * v, axis=0, keepdims=True)
    a, b, c = (p.astype(f32) for p in three_parts(half))
    row = lax.broadcasted_iota(jnp.int32, (16, v.shape[1]), 0)
    base = 0 if left else 3
    ones = jnp.where((row >= 3 - base) & (row < 6 - base), 1.0, 0.0)
    tail = jnp.where(row == base, a, jnp.where(row == base + 1, b, jnp.where(row == base + 2, c, ones)))
    tail = tail.astype(bf16)
    if left:
        parts = [high, high, mid, high, low, mid, tail]
    else:
        parts = [high, mid, high, low, high, mid, tail]
    return jnp.concatenate(parts, axis=0)


def spread_block(f_ref, b_ref, x_ref, y_ref):
    width = f_ref.shape[0]
    values = f_ref[...]
    for i in range(x_ref.shape[0]):
        x_ref[i] = values
    y_ref[:width] = values
    y_ref[width:] = b_ref[...]


def kernel_block(gain, x_ref, y_ref, k_ref, q_ref, col_ref, right_ref):
    count, size, width = x_ref.shape
    total = k_ref.shape[1]
    y = jnp.concatenate([y_ref[i, :size] for i in range(count)], axis=1) * gain
    right_ref[...] = extended(y, False)
    step = 512
    col_ref[...] = jnp.zeros_like(col_ref)
    for i in range(count):
        left = extended(x_ref[i] * gain, True)
        lanes = jnp.zeros((width, 128), f32)
        for j in range(0, total, step):
            expo = lax.dot_general(
                left, right_ref[:, j : j + step], (((0,), (0,)), ((), ())),
                preferred_element_type=f32,
            )
            tile = jnp.exp2(expo).astype(bf16)
            k_ref[i * width : (i + 1) * width, j : j + step] = tile
            wide = tile.astype(f32)
            col_ref[:, j : j + step] += jnp.sum(wide, axis=0, keepdims=True)
            for t in range(0, step, 128):
                lanes = lanes + wide[:, t : t + 128]
        sums = jnp.sum(lanes.T, axis=0, keepdims=True)
        for d in range(count):
            q_ref[d, i : i + 1, :] = sums


def second_block(q_ref, k_ref, col_ref, out_ref):
    count, _, width = q_ref.shape
    total = k_ref.shape[1]
    inv = 1.0 / jnp.sum(q_ref[...], axis=0)
    acc = jnp.zeros((8, total), f32)
    for i in range(count):
        tall = jnp.broadcast_to(inv[i : i + 1, :], (128, width)).T
        for r in range(0, width, 16):
            rows = k_ref[i * width + r : i * width + r + 16, :].astype(f32)
            w = tall[r : r + 16, :]
            prod = jnp.concatenate(
                [rows[:, t : t + 128] * w for t in range(0, total, 128)], axis=1
            )
            acc = acc + prod[:8] + prod[8:]
    second = jnp.sum(acc, axis=0, keepdims=True)
    for d in range(count):
        out_ref[d, 0:1, :] = col_ref[...]
        out_ref[d, 1:2, :] = second


def product_block(m_ref, k_ref, b_ref, out_ref, fac_ref):
    count, rows, width = b_ref.shape
    size = rows - out_ref.shape[1]
    sums = jnp.sum(m_ref[...], axis=0)
    inv = 1.0 / sums[0:1]
    factor = inv * lax.rsqrt(sums[1:2] * inv)
    block = jnp.concatenate([b_ref[i, size:] for i in range(count)], axis=1)
    weighted = (block * factor).astype(bf16)
    for i in range(count):
        out_ref[i] = lax.dot_general(
            weighted, k_ref[i * width : (i + 1) * width, :], (((1,), (1,)), ((), ())),
            preferred_element_type=f32,
        )
        fac_ref[i] = factor[:, i * width : (i + 1) * width]


def per_device(features, block):
    width, owned = features.shape
    n = lax.axis_size(GROUP_X)
    m = lax.axis_size(GROUP_Y)
    frames = owned * n * m
    scale = 4.0 / (float(frames) ** (2.0 / width) - 1.0)
    gain = math.sqrt(2.0 * math.log2(math.e) / scale)
    k_rows, k_cols = n * owned, m * owned

    copies, both = pl.pallas_call(
        spread_block,
        out_shape=(
            jax.ShapeDtypeStruct((n, width, owned), f32),
            jax.ShapeDtypeStruct((width + block.shape[0], owned), f32),
        ),
        in_specs=[VMEM] * 2,
        out_specs=(VMEM,) * 2,
        compiler_params=PARAMS,
        name="spread_block",
    )(features, block)
    x_feat = lax.all_to_all(copies, GROUP_X, 0, 0, tiled=True)
    y_both = lax.all_gather(both, GROUP_Y)
    kern, q_parts, col_sum = pl.pallas_call(
        functools.partial(kernel_block, gain),
        out_shape=(
            jax.ShapeDtypeStruct((k_rows, k_cols), bf16),
            jax.ShapeDtypeStruct((n, n, owned), f32),
            jax.ShapeDtypeStruct((1, k_cols), f32),
        ),
        in_specs=[VMEM] * 2,
        out_specs=(VMEM,) * 3,
        scratch_shapes=[pltpu.VMEM((6 * width + 16, k_cols), bf16)],
        compiler_params=PARAMS,
        name="kernel_block",
    )(x_feat, y_both)
    q_parts = lax.all_to_all(q_parts, GROUP_X, 0, 0, tiled=True)
    sums = pl.pallas_call(
        second_block,
        out_shape=jax.ShapeDtypeStruct((m, 2, k_cols), f32),
        in_specs=[VMEM] * 3,
        out_specs=VMEM,
        compiler_params=PARAMS,
        name="second_block",
    )(q_parts, kern, col_sum)
    sums = lax.all_to_all(sums, GROUP_Y, 0, 0, tiled=True)
    parts, factor = pl.pallas_call(
        product_block,
        out_shape=(
            jax.ShapeDtypeStruct((n, block.shape[0], owned), f32),
            jax.ShapeDtypeStruct((m, 1, owned), f32),
        ),
        in_specs=[VMEM] * 3,
        out_specs=(VMEM,) * 2,
        compiler_params=PARAMS,
        name="product_block",
    )(sums, kern, y_both)
    parts = lax.all_to_all(parts, GROUP_X, 0, 0, tiled=True)
    own = lax.dynamic_index_in_dim(factor, lax.axis_index(GROUP_Y), 0, keepdims=False)
    return jnp.sum(parts, axis=0) * own


def solution(mesh):
    fine = Mesh(mesh.devices.reshape(mesh.shape["row"] // 2, 2, 2, mesh.shape["col"] // 4, 2), ALL)
    placed = P(None, ALL)
    return jax.shard_map(
        per_device, mesh=fine, in_specs=(placed, placed), out_specs=placed, check_vma=False
    )
```

```python
import functools
import math

import jax
import jax.numpy as jnp
from jax import lax
from jax.experimental import pallas as pl
from jax.experimental.pallas import tpu as pltpu
from jax.sharding import Mesh, PartitionSpec as P

f32 = jnp.float32
bf16 = jnp.bfloat16
VMEM = pl.BlockSpec(memory_space=pltpu.VMEM)
PARAMS = pltpu.CompilerParams(vmem_limit_bytes=16 * 1024 * 1024)

ALL = ("z", "ylo", "yhi", "x", "core")
GROUP_X = ("ylo", "x", "core")
GROUP_Y = ("z", "yhi")


def place_in(axes):
    place = 0
    for name in axes:
        place = place * lax.axis_size(name) + lax.axis_index(name)
    return place


def three_parts(v):
    high = v.astype(bf16)
    rest = v - high.astype(f32)
    mid = rest.astype(bf16)
    low = (rest - mid.astype(f32)).astype(bf16)
    return high, mid, low


def extended(v, left):
    high, mid, low = three_parts(v)
    half = -0.5 * jnp.sum(v * v, axis=0, keepdims=True)
    a, b, c = (p.astype(f32) for p in three_parts(half))
    row = lax.broadcasted_iota(jnp.int32, (16, v.shape[1]), 0)
    base = 0 if left else 3
    ones = jnp.where((row >= 3 - base) & (row < 6 - base), 1.0, 0.0)
    tail = jnp.where(row == base, a, jnp.where(row == base + 1, b, jnp.where(row == base + 2, c, ones)))
    tail = tail.astype(bf16)
    if left:
        parts = [high, high, mid, high, low, mid, tail]
    else:
        parts = [high, mid, high, low, high, mid, tail]
    return jnp.concatenate(parts, axis=0)


def spread_block(f_ref, b_ref, y_ref, f_here, b_here, sems):
    width = f_ref.shape[0]
    first = pltpu.make_async_copy(f_ref, f_here, sems.at[0])
    second = pltpu.make_async_copy(b_ref, b_here, sems.at[1])
    first.start()
    second.start()
    first.wait()
    second.wait()
    values = jnp.concatenate([f_here[...], b_here[...]], axis=0)
    for i in range(y_ref.shape[0]):
        y_ref[i] = values


def kernel_block(gain, near_ref, far_ref, y_ref, k_ref, q_ref, col_ref, right_ref):
    half, size, width = near_ref.shape
    count = 2 * half
    me = place_in(GROUP_X)
    total = k_ref.shape[1]
    y = jnp.concatenate([y_ref[i, :size] for i in range(count)], axis=1) * gain
    right_ref[...] = extended(y, False)
    step = 512
    col_ref[...] = jnp.zeros_like(col_ref)
    for s in range(count):
        frames = near_ref[s] if s < half else far_ref[s - half]
        left = extended(frames * gain, True)
        i = jnp.bitwise_xor(me, s)
        rows = pl.ds(pl.multiple_of(i * width, 32), width)
        lanes = jnp.zeros((width, 128), f32)
        for j in range(0, total, step):
            expo = lax.dot_general(
                left, right_ref[:, j : j + step], (((0,), (0,)), ((), ())),
                preferred_element_type=f32,
            )
            tile = jnp.exp2(expo).astype(bf16)
            k_ref[rows, j : j + step] = tile
            wide = tile.astype(f32)
            col_ref[:, j : j + step] += jnp.sum(wide, axis=0, keepdims=True)
            for t in range(0, step, 128):
                lanes = lanes + wide[:, t : t + 128]
        sums = jnp.sum(lanes.T, axis=0, keepdims=True)
        for d in range(count):
            q_ref[d, pl.ds(i, 1), :] = sums


def second_block(q_ref, k_ref, col_ref, out_ref):
    count, _, width = q_ref.shape
    total = k_ref.shape[1]
    inv = 1.0 / jnp.sum(q_ref[...], axis=0)
    acc = jnp.zeros((8, total), f32)
    for i in range(count):
        tall = jnp.broadcast_to(inv[i : i + 1, :], (128, width)).T
        for r in range(0, width, 16):
            rows = k_ref[i * width + r : i * width + r + 16, :].astype(f32)
            w = tall[r : r + 16, :]
            prod = jnp.concatenate(
                [rows[:, t : t + 128] * w for t in range(0, total, 128)], axis=1
            )
            acc = acc + prod[:8] + prod[8:]
    second = jnp.sum(acc, axis=0, keepdims=True)
    for d in range(count):
        out_ref[d, 0:1, :] = col_ref[...]
        out_ref[d, 1:2, :] = second


def product_block(m_ref, k_ref, b_ref, out_ref, own_ref, fac_ref):
    count, rows, width = b_ref.shape
    size = rows - out_ref.shape[1]
    sums = jnp.sum(m_ref[...], axis=0)
    inv = 1.0 / sums[0:1]
    factor = inv * lax.rsqrt(sums[1:2] * inv)
    block = jnp.concatenate([b_ref[i, size:] for i in range(count)], axis=1)
    weighted = (block * factor).astype(bf16)
    for i in range(count):
        out_ref[i] = lax.dot_general(
            weighted, k_ref[i * width : (i + 1) * width, :], (((1,), (1,)), ((), ())),
            preferred_element_type=f32,
        )
        fac_ref[i] = factor[:, i * width : (i + 1) * width]
    own_ref[...] = fac_ref[place_in(GROUP_Y)]


def per_device(features, block):
    width, owned = features.shape
    n = lax.axis_size(GROUP_X)
    m = lax.axis_size(GROUP_Y)
    frames = owned * n * m
    scale = 4.0 / (float(frames) ** (2.0 / width) - 1.0)
    gain = math.sqrt(2.0 * math.log2(math.e) / scale)
    k_rows, k_cols = n * owned, m * owned

    held = features[None]
    received = held
    for axis, step in (("core", 1), ("x", 1), ("x", 2), ("ylo", 1)):
        pairs = [(k, k ^ step) for k in range(lax.axis_size(axis))]
        if received is not held:
            held = jnp.concatenate([held, received], axis=0)
        received = lax.ppermute(held, axis, pairs)
    copies = pl.pallas_call(
        spread_block,
        out_shape=jax.ShapeDtypeStruct((m, width + block.shape[0], owned), f32),
        in_specs=[pl.BlockSpec(memory_space=pltpu.HBM)] * 2,
        out_specs=VMEM,
        scratch_shapes=[
            pltpu.VMEM((width, owned), f32),
            pltpu.VMEM(block.shape, f32),
            pltpu.SemaphoreType.DMA((2,)),
        ],
        compiler_params=PARAMS,
        name="spread_block",
    )(features, block)
    y_both = lax.all_to_all(copies, GROUP_Y, 0, 0, tiled=True)
    kern, q_parts, col_sum = pl.pallas_call(
        functools.partial(kernel_block, gain),
        out_shape=(
            jax.ShapeDtypeStruct((k_rows, k_cols), bf16),
            jax.ShapeDtypeStruct((n, n, owned), f32),
            jax.ShapeDtypeStruct((1, k_cols), f32),
        ),
        in_specs=[VMEM] * 3,
        out_specs=(VMEM,) * 3,
        scratch_shapes=[pltpu.VMEM((6 * width + 16, k_cols), bf16)],
        compiler_params=PARAMS,
        name="kernel_block",
    )(held, received, y_both)
    q_parts = lax.all_to_all(q_parts, GROUP_X, 0, 0, tiled=True)
    sums = pl.pallas_call(
        second_block,
        out_shape=jax.ShapeDtypeStruct((m, 2, k_cols), f32),
        in_specs=[VMEM] * 3,
        out_specs=VMEM,
        compiler_params=PARAMS,
        name="second_block",
    )(q_parts, kern, col_sum)
    sums = lax.all_to_all(sums, GROUP_Y, 0, 0, tiled=True)
    parts, factor = pl.pallas_call(
        product_block,
        out_shape=(
            jax.ShapeDtypeStruct((n, block.shape[0], owned), f32),
            jax.ShapeDtypeStruct((1, owned), f32),
        ),
        in_specs=[VMEM] * 3,
        out_specs=(VMEM,) * 2,
        scratch_shapes=[pltpu.VMEM((m, 1, owned), f32)],
        compiler_params=PARAMS,
        name="product_block",
    )(sums, kern, y_both)
    parts = lax.all_to_all(parts, GROUP_X, 0, 0, tiled=True)
    return jnp.sum(parts, axis=0) * factor


def solution(mesh):
    fine = Mesh(mesh.devices.reshape(mesh.shape["row"] // 2, 2, 2, mesh.shape["col"] // 4, 2), ALL)
    placed = P(None, ALL)
    return jax.shard_map(
        per_device, mesh=fine, in_specs=(placed, placed), out_specs=placed, check_vma=False
    )
```

```python
import functools
import math

import jax
import jax.numpy as jnp
from jax import lax
from jax.experimental import pallas as pl
from jax.experimental.pallas import tpu as pltpu
from jax.sharding import Mesh, PartitionSpec as P

f32 = jnp.float32
bf16 = jnp.bfloat16
VMEM = pl.BlockSpec(memory_space=pltpu.VMEM)
PARAMS = pltpu.CompilerParams(vmem_limit_bytes=16 * 1024 * 1024)

ALL = ("z", "ylo", "yhi", "x", "core")
GROUP_X = ("ylo", "yhi", "x")
GROUP_Y = ("z", "core")


def place_in(axes):
    place = 0
    for name in axes:
        place = place * lax.axis_size(name) + lax.axis_index(name)
    return place


def three_parts(v):
    high = v.astype(bf16)
    rest = v - high.astype(f32)
    mid = rest.astype(bf16)
    low = (rest - mid.astype(f32)).astype(bf16)
    return high, mid, low


def extended(v, left):
    high, mid, low = three_parts(v)
    half = -0.5 * jnp.sum(v * v, axis=0, keepdims=True)
    a, b, c = (p.astype(f32) for p in three_parts(half))
    row = lax.broadcasted_iota(jnp.int32, (16, v.shape[1]), 0)
    base = 0 if left else 3
    ones = jnp.where((row >= 3 - base) & (row < 6 - base), 1.0, 0.0)
    tail = jnp.where(row == base, a, jnp.where(row == base + 1, b, jnp.where(row == base + 2, c, ones)))
    tail = tail.astype(bf16)
    if left:
        parts = [high, high, mid, high, low, mid, tail]
    else:
        parts = [high, mid, high, low, high, mid, tail]
    return jnp.concatenate(parts, axis=0)


def spread_block(f_ref, b_ref, x_ref, y_ref):
    width = f_ref.shape[0]
    values = f_ref[...]
    for i in range(x_ref.shape[0]):
        x_ref[i] = values
    y_ref[:width] = values
    y_ref[width:] = b_ref[...]


def kernel_block(gain, x_ref, y_ref, k_ref, q_ref, col_ref, right_ref):
    count, size, width = x_ref.shape
    total = k_ref.shape[1]
    y = jnp.concatenate([y_ref[i, :size] for i in range(count)], axis=1) * gain
    right_ref[...] = extended(y, False)
    step = 512
    col_ref[...] = jnp.zeros_like(col_ref)
    for i in range(count):
        left = extended(x_ref[i] * gain, True)
        rows = slice(i * width, (i + 1) * width)
        lanes = jnp.zeros((width, 128), f32)
        for j in range(0, total, step):
            expo = lax.dot_general(
                left, right_ref[:, j : j + step], (((0,), (0,)), ((), ())),
                preferred_element_type=f32,
            )
            tile = jnp.exp2(expo).astype(bf16)
            k_ref[rows, j : j + step] = tile
            wide = tile.astype(f32)
            col_ref[:, j : j + step] += jnp.sum(wide, axis=0, keepdims=True)
            for t in range(0, step, 128):
                lanes = lanes + wide[:, t : t + 128]
        sums = jnp.sum(lanes.T, axis=0, keepdims=True)
        for d in range(count):
            q_ref[d, i : i + 1, :] = sums


def second_block(q_ref, k_ref, col_ref, out_ref):
    count, _, width = q_ref.shape
    total = k_ref.shape[1]
    inv = 1.0 / jnp.sum(q_ref[...], axis=0)
    acc = jnp.zeros((8, total), f32)
    for i in range(count):
        tall = jnp.broadcast_to(inv[i : i + 1, :], (128, width)).T
        for r in range(0, width, 16):
            rows = k_ref[i * width + r : i * width + r + 16, :].astype(f32)
            w = tall[r : r + 16, :]
            prod = jnp.concatenate(
                [rows[:, t : t + 128] * w for t in range(0, total, 128)], axis=1
            )
            acc = acc + prod[:8] + prod[8:]
    second = jnp.sum(acc, axis=0, keepdims=True)
    for d in range(count):
        out_ref[d, 0:1, :] = col_ref[...]
        out_ref[d, 1:2, :] = second


def product_block(m_ref, k_ref, b_ref, out_ref, own_ref, fac_ref):
    count, rows, width = b_ref.shape
    size = rows - out_ref.shape[1]
    sums = jnp.sum(m_ref[...], axis=0)
    inv = 1.0 / sums[0:1]
    factor = inv * lax.rsqrt(sums[1:2] * inv)
    block = jnp.concatenate([b_ref[i, size:] for i in range(count)], axis=1)
    weighted = (block * factor).astype(bf16)
    for i in range(count):
        out_ref[i] = lax.dot_general(
            weighted, k_ref[i * width : (i + 1) * width, :], (((1,), (1,)), ((), ())),
            preferred_element_type=f32,
        )
        fac_ref[i] = factor[:, i * width : (i + 1) * width]
    own_ref[...] = fac_ref[place_in(GROUP_Y)]


def per_device(features, block):
    width, owned = features.shape
    n = lax.axis_size(GROUP_X)
    m = lax.axis_size(GROUP_Y)
    frames = owned * n * m
    scale = 4.0 / (float(frames) ** (2.0 / width) - 1.0)
    gain = math.sqrt(2.0 * math.log2(math.e) / scale)
    k_rows, k_cols = n * owned, m * owned

    copies, both = pl.pallas_call(
        spread_block,
        out_shape=(
            jax.ShapeDtypeStruct((n, width, owned), f32),
            jax.ShapeDtypeStruct((width + block.shape[0], owned), f32),
        ),
        in_specs=[VMEM] * 2,
        out_specs=(VMEM,) * 2,
        compiler_params=PARAMS,
        name="spread_block",
    )(features, block)
    x_feat = lax.all_to_all(copies, GROUP_X, 0, 0, tiled=True)
    y_both = lax.all_gather(both, GROUP_Y)
    kern, q_parts, col_sum = pl.pallas_call(
        functools.partial(kernel_block, gain),
        out_shape=(
            jax.ShapeDtypeStruct((k_rows, k_cols), bf16),
            jax.ShapeDtypeStruct((n, n, owned), f32),
            jax.ShapeDtypeStruct((1, k_cols), f32),
        ),
        in_specs=[VMEM] * 2,
        out_specs=(VMEM,) * 3,
        scratch_shapes=[pltpu.VMEM((6 * width + 16, k_cols), bf16)],
        compiler_params=PARAMS,
        name="kernel_block",
    )(x_feat, y_both)
    q_parts = lax.all_to_all(q_parts, GROUP_X, 0, 0, tiled=True)
    sums = pl.pallas_call(
        second_block,
        out_shape=jax.ShapeDtypeStruct((m, 2, k_cols), f32),
        in_specs=[VMEM] * 3,
        out_specs=VMEM,
        compiler_params=PARAMS,
        name="second_block",
    )(q_parts, kern, col_sum)
    sums = lax.all_to_all(sums, GROUP_Y, 0, 0, tiled=True)
    parts, factor = pl.pallas_call(
        product_block,
        out_shape=(
            jax.ShapeDtypeStruct((n, block.shape[0], owned), f32),
            jax.ShapeDtypeStruct((1, owned), f32),
        ),
        in_specs=[VMEM] * 3,
        out_specs=(VMEM,) * 2,
        scratch_shapes=[pltpu.VMEM((m, 1, owned), f32)],
        compiler_params=PARAMS,
        name="product_block",
    )(sums, kern, y_both)
    parts = lax.all_to_all(parts, GROUP_X, 0, 0, tiled=True)
    return jnp.sum(parts, axis=0) * factor


def solution(mesh):
    fine = Mesh(mesh.devices.reshape(mesh.shape["row"] // 2, 2, 2, mesh.shape["col"] // 4, 2), ALL)
    placed = P(None, ALL)
    return jax.shard_map(
        per_device, mesh=fine, in_specs=(placed, placed), out_specs=placed, check_vma=False
    )
```

```python
import functools
import math

import jax
import jax.numpy as jnp
from jax import lax
from jax.experimental import pallas as pl
from jax.experimental.pallas import tpu as pltpu
from jax.sharding import Mesh, PartitionSpec as P

f32 = jnp.float32
bf16 = jnp.bfloat16
VMEM = pl.BlockSpec(memory_space=pltpu.VMEM)
PARAMS = pltpu.CompilerParams(vmem_limit_bytes=16 * 1024 * 1024)

ALL = ("z", "ylo", "yhi", "x", "core")
GROUP_X = ("ylo", "yhi", "x")
GROUP_Y = ("z", "core")


def place_in(axes):
    place = 0
    for name in axes:
        place = place * lax.axis_size(name) + lax.axis_index(name)
    return place


def three_parts(v):
    high = v.astype(bf16)
    rest = v - high.astype(f32)
    mid = rest.astype(bf16)
    low = (rest - mid.astype(f32)).astype(bf16)
    return high, mid, low


def extended(v, left):
    high, mid, low = three_parts(v)
    half = -0.5 * jnp.sum(v * v, axis=0, keepdims=True)
    a, b, c = (p.astype(f32) for p in three_parts(half))
    row = lax.broadcasted_iota(jnp.int32, (16, v.shape[1]), 0)
    base = 0 if left else 3
    ones = jnp.where((row >= 3 - base) & (row < 6 - base), 1.0, 0.0)
    tail = jnp.where(row == base, a, jnp.where(row == base + 1, b, jnp.where(row == base + 2, c, ones)))
    tail = tail.astype(bf16)
    if left:
        parts = [high, high, mid, high, low, mid, tail]
    else:
        parts = [high, mid, high, low, high, mid, tail]
    return jnp.concatenate(parts, axis=0)


def spread_block(f_ref, b_ref, x_ref, y_ref, here, in_sem, x_sem, y_sem):
    width = f_ref.shape[0]
    fetch = pltpu.make_async_copy(f_ref, here, in_sem)
    fetch.start()
    lower = pltpu.make_async_copy(f_ref, y_ref.at[pl.ds(0, width)], y_sem.at[0])
    upper = pltpu.make_async_copy(b_ref, y_ref.at[pl.ds(width, b_ref.shape[0])], y_sem.at[1])
    lower.start()
    upper.start()
    fetch.wait()
    copies = [
        pltpu.make_async_copy(here, x_ref.at[i], x_sem.at[i]) for i in range(x_ref.shape[0])
    ]
    for copy in copies:
        copy.start()
    for copy in copies:
        copy.wait()
    lower.wait()
    upper.wait()


def kernel_block(gain, x_ref, y_ref, k_ref, q_ref, right_ref):
    count, size, width = x_ref.shape
    total = k_ref.shape[1]
    y = jnp.concatenate([y_ref[i, :size] for i in range(count)], axis=1) * gain
    right_ref[...] = extended(y, False)
    step = 512
    for i in range(count):
        left = extended(x_ref[i] * gain, True)
        rows = slice(i * width, (i + 1) * width)
        lanes = jnp.zeros((width, 128), f32)
        for j in range(0, total, step):
            expo = lax.dot_general(
                left, right_ref[:, j : j + step], (((0,), (0,)), ((), ())),
                preferred_element_type=f32,
            )
            tile = jnp.exp2(expo).astype(bf16)
            k_ref[rows, j : j + step] = tile
            wide = tile.astype(f32)
            for t in range(0, step, 128):
                lanes = lanes + wide[:, t : t + 128]
        sums = jnp.sum(lanes.T, axis=0, keepdims=True)
        for d in range(count):
            q_ref[d, i : i + 1, :] = sums


def second_block(q_ref, k_ref, out_ref, sum_ref, line_ref):
    line_ref[...] = jnp.zeros_like(line_ref)
    count, _, width = q_ref.shape
    total = k_ref.shape[1]
    q = jnp.sum(q_ref[...], axis=0)
    sum_ref[...] = q
    own = sum_ref[pl.ds(place_in(GROUP_X), 1), :]
    inv = 1.0 / q
    acc = jnp.zeros((8, total), f32)
    for i in range(count):
        tall = jnp.broadcast_to(inv[i : i + 1, :], (128, width)).T
        for r in range(0, width, 16):
            rows = k_ref[i * width + r : i * width + r + 16, :].astype(f32)
            w = tall[r : r + 16, :]
            prod = jnp.concatenate(
                [rows[:, t : t + 128] * w for t in range(0, total, 128)], axis=1
            )
            acc = acc + prod[:8] + prod[8:]
    second = jnp.sum(acc, axis=0, keepdims=True)
    mine = place_in(GROUP_Y)
    second = second - jnp.concatenate(
        [jnp.where(mine == i, 1.0 / own, 0.0) for i in range(total // width)], axis=1
    )
    second = second * (1.0 + mine.astype(f32) / out_ref.shape[0])
    lines = total // 128
    for i in range(lines):
        line_ref[i : i + 1, :] = second[:, i * 128 : (i + 1) * 128]
    for i, part in enumerate(three_parts(own)):
        line_ref[lines + i : lines + i + 1, :width] = part.astype(f32)
    message = line_ref[...].astype(bf16)
    for d in range(out_ref.shape[0]):
        out_ref[d] = message


def product_block(m_ref, k_ref, b_ref, out_ref, own_ref, add_ref, fac_ref, line_ref):
    count, rows, width = b_ref.shape
    size = rows - out_ref.shape[1]
    lines = k_ref.shape[1] // 128
    summed = m_ref[0].astype(f32)
    line_ref[0] = summed
    for i in range(1, count):
        lined = m_ref[i].astype(f32)
        line_ref[i] = lined
        summed = summed + lined * (1.0 / (1.0 + i / count))
    q = jnp.concatenate(
        [
            line_ref[i, lines : lines + 1, :width]
            + line_ref[i, lines + 1 : lines + 2, :width]
            + line_ref[i, lines + 2 : lines + 3, :width]
            for i in range(count)
        ],
        axis=1,
    )
    line_ref[0] = summed
    second = jnp.concatenate([line_ref[0, i : i + 1, :] for i in range(lines)], axis=1)
    inv = 1.0 / q
    second = second + inv
    factor = inv * lax.rsqrt(second * inv)
    block = jnp.concatenate([b_ref[i, size:] for i in range(count)], axis=1)
    weighted = (block * factor).astype(bf16)
    for i in range(count):
        fac_ref[i] = factor[:, i * width : (i + 1) * width]
    place, mine = place_in(GROUP_X), place_in(GROUP_Y)
    own = fac_ref[mine]
    own_ref[...] = own
    added = (b_ref[mine, size:] * own).astype(bf16).astype(f32)
    add_ref[...] = added
    for i in range(out_ref.shape[0]):
        value = lax.dot_general(
            weighted, k_ref[i * width : (i + 1) * width, :], (((1,), (1,)), ((), ())),
            preferred_element_type=f32,
        )
        out_ref[i] = jnp.where(place == i, value - added, value).astype(bf16)


def per_device(features, block):
    width, owned = features.shape
    n = lax.axis_size(GROUP_X)
    m = lax.axis_size(GROUP_Y)
    frames = owned * n * m
    scale = 4.0 / (float(frames) ** (2.0 / width) - 1.0)
    gain = math.sqrt(2.0 * math.log2(math.e) / scale)
    k_rows, k_cols = n * owned, m * owned
    lines = pl.cdiv(k_cols // 128 + 3, 16) * 16

    anywhere = pl.BlockSpec(memory_space=pl.ANY)
    copies, both = pl.pallas_call(
        spread_block,
        out_shape=(
            jax.ShapeDtypeStruct((n, width, owned), f32),
            jax.ShapeDtypeStruct((width + block.shape[0], owned), f32),
        ),
        in_specs=[anywhere] * 2,
        out_specs=(anywhere,) * 2,
        scratch_shapes=[
            pltpu.VMEM((width, owned), f32),
            pltpu.SemaphoreType.DMA,
            pltpu.SemaphoreType.DMA((n,)),
            pltpu.SemaphoreType.DMA((2,)),
        ],
        cost_estimate=pl.CostEstimate(flops=0, bytes_accessed=0, transcendentals=0),
        compiler_params=PARAMS,
        name="spread_block",
    )(*(pltpu.with_memory_space_constraint(a, pltpu.HBM) for a in (features, block)))
    x_feat = lax.all_to_all(copies, GROUP_X, 0, 0, tiled=True)
    y_both = lax.all_gather(both, GROUP_Y)
    kern, q_parts = pl.pallas_call(
        functools.partial(kernel_block, gain),
        out_shape=(
            jax.ShapeDtypeStruct((k_rows, k_cols), bf16),
            jax.ShapeDtypeStruct((n, n, owned), f32),
        ),
        in_specs=[VMEM] * 2,
        out_specs=(VMEM,) * 2,
        scratch_shapes=[pltpu.VMEM((6 * width + 16, k_cols), bf16)],
        compiler_params=PARAMS,
        name="kernel_block",
    )(x_feat, y_both)
    q_parts = lax.all_to_all(q_parts, GROUP_X, 0, 0, tiled=True)
    sums = pl.pallas_call(
        second_block,
        out_shape=jax.ShapeDtypeStruct((m, lines, 128), bf16),
        in_specs=[VMEM] * 2,
        out_specs=VMEM,
        scratch_shapes=[pltpu.VMEM((n, owned), f32), pltpu.VMEM((lines, 128), f32)],
        compiler_params=PARAMS,
        name="second_block",
    )(q_parts, kern)
    sums = lax.all_to_all(sums, GROUP_Y, 0, 0, tiled=True)
    parts, factor, diagonal = pl.pallas_call(
        product_block,
        out_shape=(
            jax.ShapeDtypeStruct((n, block.shape[0], owned), bf16),
            jax.ShapeDtypeStruct((1, owned), f32),
            jax.ShapeDtypeStruct(block.shape, f32),
        ),
        in_specs=[VMEM] * 3,
        out_specs=(VMEM,) * 3,
        scratch_shapes=[pltpu.VMEM((m, 1, owned), f32), pltpu.VMEM((m, lines, 128), f32)],
        compiler_params=PARAMS,
        name="product_block",
    )(sums, kern, y_both)
    parts = lax.all_to_all(parts, GROUP_X, 0, 0, tiled=True)
    return (jnp.sum(parts.astype(f32), axis=0) + diagonal) * factor


def solution(mesh):
    fine = Mesh(mesh.devices.reshape(mesh.shape["row"] // 2, 2, 2, mesh.shape["col"] // 4, 2), ALL)
    placed = P(None, ALL)
    return jax.shard_map(
        per_device, mesh=fine, in_specs=(placed, placed), out_specs=placed, check_vma=False
    )
```

```python
import functools
import math

import jax
import jax.numpy as jnp
from jax import lax
from jax.experimental import pallas as pl
from jax.experimental.pallas import tpu as pltpu
from jax.sharding import Mesh, PartitionSpec as P

f32 = jnp.float32
bf16 = jnp.bfloat16
VMEM = pl.BlockSpec(memory_space=pltpu.VMEM)
PARAMS = pltpu.CompilerParams(vmem_limit_bytes=16 * 1024 * 1024)

ALL = ("z", "ylo", "yhi", "x", "core")
GROUP_X = ("ylo", "yhi", "x")
GROUP_Y = ("z", "core")


def place_in(axes):
    place = 0
    for name in axes:
        place = place * lax.axis_size(name) + lax.axis_index(name)
    return place


def three_parts(v):
    high = v.astype(bf16)
    rest = v - high.astype(f32)
    mid = rest.astype(bf16)
    low = (rest - mid.astype(f32)).astype(bf16)
    return high, mid, low


def extended(v, left):
    high, mid, low = three_parts(v)
    half = -0.5 * jnp.sum(v * v, axis=0, keepdims=True)
    a, b, c = (p.astype(f32) for p in three_parts(half))
    row = lax.broadcasted_iota(jnp.int32, (16, v.shape[1]), 0)
    base = 0 if left else 3
    ones = jnp.where((row >= 3 - base) & (row < 6 - base), 1.0, 0.0)
    tail = jnp.where(row == base, a, jnp.where(row == base + 1, b, jnp.where(row == base + 2, c, ones)))
    tail = tail.astype(bf16)
    if left:
        parts = [high, high, mid, high, low, mid, tail]
    else:
        parts = [high, mid, high, low, high, mid, tail]
    return jnp.concatenate(parts, axis=0)


def spread_block(f_ref, b_ref, x_ref, y_ref, here, in_sem, x_sem, y_sem):
    width = f_ref.shape[0]
    fetch = pltpu.make_async_copy(f_ref, here, in_sem)
    fetch.start()
    lower = pltpu.make_async_copy(f_ref, y_ref.at[pl.ds(0, width)], y_sem.at[0])
    upper = pltpu.make_async_copy(b_ref, y_ref.at[pl.ds(width, b_ref.shape[0])], y_sem.at[1])
    lower.start()
    upper.start()
    fetch.wait()
    copies = [
        pltpu.make_async_copy(here, x_ref.at[i], x_sem.at[i]) for i in range(x_ref.shape[0])
    ]
    for copy in copies:
        copy.start()
    for copy in copies:
        copy.wait()
    lower.wait()
    upper.wait()


def kernel_block(gain, x_ref, y_ref, k_ref, q_ref, right_ref):
    count, size, width = x_ref.shape
    total = k_ref.shape[1]
    x = jnp.concatenate([x_ref[i] for i in range(count)], axis=1) * gain
    right_ref[...] = extended(x, False)
    step = 512
    sums = [jnp.zeros((8, step), f32) for _ in range(0, total, step)]
    for i in range(y_ref.shape[0]):
        left = extended(y_ref[i, :size] * gain, True)
        for j in range(0, total, step):
            expo = lax.dot_general(
                left, right_ref[:, j : j + step], (((0,), (0,)), ((), ())),
                preferred_element_type=f32,
            )
            tile = jnp.exp2(expo).astype(bf16)
            k_ref[i * width : (i + 1) * width, j : j + step] = tile
            wide = tile.astype(f32)
            part = sums[j // step]
            for r in range(0, width, 8):
                part = part + wide[r : r + 8]
            sums[j // step] = part
    flat = jnp.sum(jnp.concatenate(sums, axis=1), axis=0, keepdims=True)
    for d in range(q_ref.shape[0]):
        q_ref[d] = flat


def second_block(q_ref, k_ref, out_ref, sum_ref, line_ref):
    line_ref[...] = jnp.zeros_like(line_ref)
    count, _, total = q_ref.shape
    width = sum_ref.shape[2]
    q = q_ref[0]
    for i in range(1, count):
        q = q + q_ref[i]
    for i in range(count):
        sum_ref[i] = q[:, i * width : (i + 1) * width]
    own = sum_ref[place_in(GROUP_X)]
    inv = 1.0 / q
    pieces = [jnp.broadcast_to(inv[:, t : t + 128], (16, 128)) for t in range(0, total, 128)]
    mine = place_in(GROUP_Y)
    apart = jnp.concatenate(
        [jnp.where(mine == i, 1.0 / own, 0.0) for i in range(k_ref.shape[0] // width)], axis=1
    )
    grade = 1.0 + mine.astype(f32) / out_ref.shape[0]
    lines = k_ref.shape[0] // 128
    for i in range(lines):
        groups = []
        for r in range(0, 128, 16):
            acc = jnp.zeros((16, 128), f32)
            for t, piece in enumerate(pieces):
                rows = k_ref[i * 128 + r : i * 128 + r + 16, t * 128 : (t + 1) * 128]
                acc = acc + rows.astype(f32) * piece
            groups.append(acc)
        line = jnp.sum(jnp.concatenate(groups, axis=0).T, axis=0, keepdims=True)
        line_ref[i : i + 1, :] = (line - apart[:, i * 128 : (i + 1) * 128]) * grade
    for i, part in enumerate(three_parts(own)):
        line_ref[lines + i : lines + i + 1, :width] = part.astype(f32)
    message = line_ref[...].astype(bf16)
    for d in range(out_ref.shape[0]):
        out_ref[d] = message


def product_block(m_ref, k_ref, b_ref, out_ref, own_ref, add_ref, fac_ref, line_ref):
    count, rows, width = b_ref.shape
    size = rows - out_ref.shape[1]
    lines = k_ref.shape[0] // 128
    summed = m_ref[0].astype(f32)
    line_ref[0] = summed
    for i in range(1, count):
        lined = m_ref[i].astype(f32)
        line_ref[i] = lined
        summed = summed + lined * (1.0 / (1.0 + i / count))
    q = jnp.concatenate(
        [
            line_ref[i, lines : lines + 1, :width]
            + line_ref[i, lines + 1 : lines + 2, :width]
            + line_ref[i, lines + 2 : lines + 3, :width]
            for i in range(count)
        ],
        axis=1,
    )
    line_ref[0] = summed
    second = jnp.concatenate([line_ref[0, i : i + 1, :] for i in range(lines)], axis=1)
    inv = 1.0 / q
    second = second + inv
    factor = inv * lax.rsqrt(second * inv)
    block = jnp.concatenate([b_ref[i, size:] for i in range(count)], axis=1)
    weighted = (block * factor).astype(bf16)
    for i in range(count):
        fac_ref[i] = factor[:, i * width : (i + 1) * width]
    place, mine = place_in(GROUP_X), place_in(GROUP_Y)
    own = fac_ref[mine]
    own_ref[...] = own
    added = (b_ref[mine, size:] * own).astype(bf16).astype(f32)
    add_ref[...] = added
    step = 512
    values = jnp.concatenate(
        [
            jnp.dot(weighted, k_ref[:, j : j + step], preferred_element_type=f32)
            for j in range(0, k_ref.shape[1], step)
        ],
        axis=1,
    )
    for i in range(out_ref.shape[0]):
        value = values[:, i * width : (i + 1) * width]
        out_ref[i] = jnp.where(place == i, value - added, value).astype(bf16)


def per_device(features, block):
    width, owned = features.shape
    n = lax.axis_size(GROUP_X)
    m = lax.axis_size(GROUP_Y)
    frames = owned * n * m
    scale = 4.0 / (float(frames) ** (2.0 / width) - 1.0)
    gain = math.sqrt(2.0 * math.log2(math.e) / scale)
    x_total, y_total = n * owned, m * owned
    lines = pl.cdiv(y_total // 128 + 3, 16) * 16

    anywhere = pl.BlockSpec(memory_space=pl.ANY)
    copies, both = pl.pallas_call(
        spread_block,
        out_shape=(
            jax.ShapeDtypeStruct((n, width, owned), f32),
            jax.ShapeDtypeStruct((width + block.shape[0], owned), f32),
        ),
        in_specs=[anywhere] * 2,
        out_specs=(anywhere,) * 2,
        scratch_shapes=[
            pltpu.VMEM((width, owned), f32),
            pltpu.SemaphoreType.DMA,
            pltpu.SemaphoreType.DMA((n,)),
            pltpu.SemaphoreType.DMA((2,)),
        ],
        cost_estimate=pl.CostEstimate(flops=0, bytes_accessed=0, transcendentals=0),
        compiler_params=PARAMS,
        name="spread_block",
    )(*(pltpu.with_memory_space_constraint(a, pltpu.HBM) for a in (features, block)))
    x_feat = lax.all_to_all(copies, GROUP_X, 0, 0, tiled=True)
    y_both = lax.all_gather(both, GROUP_Y)
    kern, q_parts = pl.pallas_call(
        functools.partial(kernel_block, gain),
        out_shape=(
            jax.ShapeDtypeStruct((y_total, x_total), bf16),
            jax.ShapeDtypeStruct((n, 1, x_total), f32),
        ),
        in_specs=[VMEM] * 2,
        out_specs=(VMEM,) * 2,
        scratch_shapes=[pltpu.VMEM((6 * width + 16, x_total), bf16)],
        compiler_params=PARAMS,
        name="kernel_block",
    )(x_feat, y_both)
    q_parts = lax.all_to_all(q_parts, GROUP_X, 0, 0, tiled=True)
    sums = pl.pallas_call(
        second_block,
        out_shape=jax.ShapeDtypeStruct((m, lines, 128), bf16),
        in_specs=[VMEM] * 2,
        out_specs=VMEM,
        scratch_shapes=[pltpu.VMEM((n, 1, owned), f32), pltpu.VMEM((lines, 128), f32)],
        compiler_params=PARAMS,
        name="second_block",
    )(q_parts, kern)
    sums = lax.all_to_all(sums, GROUP_Y, 0, 0, tiled=True)
    parts, factor, diagonal = pl.pallas_call(
        product_block,
        out_shape=(
            jax.ShapeDtypeStruct((n, block.shape[0], owned), bf16),
            jax.ShapeDtypeStruct((1, owned), f32),
            jax.ShapeDtypeStruct(block.shape, f32),
        ),
        in_specs=[VMEM] * 3,
        out_specs=(VMEM,) * 3,
        scratch_shapes=[pltpu.VMEM((m, 1, owned), f32), pltpu.VMEM((m, lines, 128), f32)],
        compiler_params=PARAMS,
        name="product_block",
    )(sums, kern, y_both)
    parts = lax.all_to_all(parts, GROUP_X, 0, 0, tiled=True)
    return (jnp.sum(parts.astype(f32), axis=0) + diagonal) * factor


def solution(mesh):
    fine = Mesh(mesh.devices.reshape(mesh.shape["row"] // 2, 2, 2, mesh.shape["col"] // 4, 2), ALL)
    placed = P(None, ALL)
    return jax.shard_map(
        per_device, mesh=fine, in_specs=(placed, placed), out_specs=placed, check_vma=False
    )
```

```python
import functools
import math

import jax
import jax.numpy as jnp
from jax import lax
from jax.experimental import pallas as pl
from jax.experimental.pallas import tpu as pltpu
from jax.sharding import Mesh, PartitionSpec as P

f32 = jnp.float32
bf16 = jnp.bfloat16
VMEM = pl.BlockSpec(memory_space=pltpu.VMEM)
PARAMS = pltpu.CompilerParams(vmem_limit_bytes=16 * 1024 * 1024)

ALL = ("z", "ylo", "yhi", "x", "core")
GROUP_X = ("ylo", "yhi", "x")
GROUP_Y = ("z", "core")


X_FIRST, Y_FIRST = 15, 0
Q_FIRST, SECOND_FIRST, PRODUCT_FIRST = 9, 12, 6


def index_in(axes):
    index = 0
    for name in axes:
        index = index * lax.axis_size(name) + lax.axis_index(name)
    return index


def listed(axes, first):
    count = math.prod(lax.axis_size(name) for name in axes)
    if axes == GROUP_Y:
        return [[(k + first) % count for k in range(count)]]
    return [[k ^ first for k in range(count)]]


def x_place():
    return jnp.bitwise_xor(index_in(GROUP_X), X_FIRST)


def y_place(count):
    return lax.rem(index_in(GROUP_Y) + count - Y_FIRST, count)


def exchanged(x, axes, first):
    return lax.all_to_all(x, axes, 0, 0, tiled=True, axis_index_groups=listed(axes, first))


def three_parts(v):
    high = v.astype(bf16)
    rest = v - high.astype(f32)
    mid = rest.astype(bf16)
    low = (rest - mid.astype(f32)).astype(bf16)
    return high, mid, low


def extended(v, left):
    high, mid, low = three_parts(v)
    half = -0.5 * jnp.sum(v * v, axis=0, keepdims=True)
    a, b, c = (p.astype(f32) for p in three_parts(half))
    row = lax.broadcasted_iota(jnp.int32, (16, v.shape[1]), 0)
    base = 0 if left else 3
    ones = jnp.where((row >= 3 - base) & (row < 6 - base), 1.0, 0.0)
    tail = jnp.where(row == base, a, jnp.where(row == base + 1, b, jnp.where(row == base + 2, c, ones)))
    tail = tail.astype(bf16)
    if left:
        parts = [high, high, mid, high, low, mid, tail]
    else:
        parts = [high, mid, high, low, high, mid, tail]
    return jnp.concatenate(parts, axis=0)


def spread_block(f_ref, b_ref, x_ref, y_ref, here, in_sem, x_sem, y_sem):
    width = f_ref.shape[0]
    fetch = pltpu.make_async_copy(f_ref, here, in_sem)
    fetch.start()
    lower = pltpu.make_async_copy(f_ref, y_ref.at[pl.ds(0, width)], y_sem.at[0])
    upper = pltpu.make_async_copy(b_ref, y_ref.at[pl.ds(width, b_ref.shape[0])], y_sem.at[1])
    lower.start()
    upper.start()
    fetch.wait()
    copies = [
        pltpu.make_async_copy(here, x_ref.at[i], x_sem.at[i]) for i in range(x_ref.shape[0])
    ]
    for copy in copies:
        copy.start()
    for copy in copies:
        copy.wait()
    lower.wait()
    upper.wait()


def kernel_block(gain, x_ref, y_ref, k_ref, q_ref, right_ref):
    count, size, width = x_ref.shape
    total = k_ref.shape[1]
    x = jnp.concatenate([x_ref[i] for i in range(count)], axis=1) * gain
    right_ref[...] = extended(x, False)
    step = 512
    sums = [jnp.zeros((8, step), f32) for _ in range(0, total, step)]
    for i in range(y_ref.shape[0]):
        left = extended(y_ref[i, :size] * gain, True)
        for j in range(0, total, step):
            expo = lax.dot_general(
                left, right_ref[:, j : j + step], (((0,), (0,)), ((), ())),
                preferred_element_type=f32,
            )
            tile = jnp.exp2(expo).astype(bf16)
            k_ref[i * width : (i + 1) * width, j : j + step] = tile
            wide = tile.astype(f32)
            part = sums[j // step]
            for r in range(0, width, 8):
                part = part + wide[r : r + 8]
            sums[j // step] = part
    flat = jnp.sum(jnp.concatenate(sums, axis=1), axis=0, keepdims=True)
    for d in range(q_ref.shape[0]):
        q_ref[d] = flat


def second_block(q_ref, k_ref, out_ref, sum_ref, line_ref):
    line_ref[...] = jnp.zeros_like(line_ref)
    count, _, total = q_ref.shape
    width = sum_ref.shape[2]
    q = q_ref[0]
    for i in range(1, count):
        q = q + q_ref[i]
    for i in range(count):
        sum_ref[i] = q[:, i * width : (i + 1) * width]
    own = sum_ref[x_place()]
    inv = 1.0 / q
    pieces = [jnp.broadcast_to(inv[:, t : t + 128], (16, 128)) for t in range(0, total, 128)]
    mine = y_place(out_ref.shape[0])
    apart = jnp.concatenate(
        [jnp.where(mine == i, 1.0 / own, 0.0) for i in range(k_ref.shape[0] // width)], axis=1
    )
    grade = 1.0 + mine.astype(f32) / out_ref.shape[0]
    lines = k_ref.shape[0] // 128
    for i in range(lines):
        groups = []
        for r in range(0, 128, 16):
            acc = jnp.zeros((16, 128), f32)
            for t, piece in enumerate(pieces):
                rows = k_ref[i * 128 + r : i * 128 + r + 16, t * 128 : (t + 1) * 128]
                acc = acc + rows.astype(f32) * piece
            groups.append(acc)
        line = jnp.sum(jnp.concatenate(groups, axis=0).T, axis=0, keepdims=True)
        line_ref[i : i + 1, :] = (line - apart[:, i * 128 : (i + 1) * 128]) * grade
    for i, part in enumerate(three_parts(own)):
        line_ref[lines + i : lines + i + 1, :width] = part.astype(f32)
    message = line_ref[...].astype(bf16)
    for d in range(out_ref.shape[0]):
        out_ref[d] = message


def product_block(m_ref, k_ref, b_ref, out_ref, own_ref, add_ref, fac_ref, line_ref):
    count, rows, width = b_ref.shape
    size = rows - out_ref.shape[1]
    lines = k_ref.shape[0] // 128
    summed = jnp.zeros(m_ref.shape[1:], f32)
    for k in range(count):
        i = (k + SECOND_FIRST - Y_FIRST) % count
        lined = m_ref[k].astype(f32)
        line_ref[i] = lined
        summed = summed + lined * (1.0 / (1.0 + i / count))
    q = jnp.concatenate(
        [
            line_ref[i, lines : lines + 1, :width]
            + line_ref[i, lines + 1 : lines + 2, :width]
            + line_ref[i, lines + 2 : lines + 3, :width]
            for i in range(count)
        ],
        axis=1,
    )
    line_ref[0] = summed
    second = jnp.concatenate([line_ref[0, i : i + 1, :] for i in range(lines)], axis=1)
    inv = 1.0 / q
    second = second + inv
    factor = inv * lax.rsqrt(second * inv)
    block = jnp.concatenate([b_ref[i, size:] for i in range(count)], axis=1)
    weighted = (block * factor).astype(bf16)
    for i in range(count):
        fac_ref[i] = factor[:, i * width : (i + 1) * width]
    place, mine = x_place(), y_place(count)
    own = fac_ref[mine]
    own_ref[...] = own
    added = (b_ref[mine, size:] * own).astype(bf16).astype(f32)
    add_ref[...] = added
    step = 512
    values = jnp.concatenate(
        [
            jnp.dot(weighted, k_ref[:, j : j + step], preferred_element_type=f32)
            for j in range(0, k_ref.shape[1], step)
        ],
        axis=1,
    )
    for i in range(out_ref.shape[0]):
        value = values[:, i * width : (i + 1) * width]
        value = jnp.where(place == i, value - added, value)
        out_ref[i ^ X_FIRST ^ PRODUCT_FIRST] = value.astype(bf16)


def per_device(features, block):
    width, owned = features.shape
    n = lax.axis_size(GROUP_X)
    m = lax.axis_size(GROUP_Y)
    frames = owned * n * m
    scale = 4.0 / (float(frames) ** (2.0 / width) - 1.0)
    gain = math.sqrt(2.0 * math.log2(math.e) / scale)
    x_total, y_total = n * owned, m * owned
    lines = pl.cdiv(y_total // 128 + 3, 16) * 16

    anywhere = pl.BlockSpec(memory_space=pl.ANY)
    copies, both = pl.pallas_call(
        spread_block,
        out_shape=(
            jax.ShapeDtypeStruct((n, width, owned), f32),
            jax.ShapeDtypeStruct((width + block.shape[0], owned), f32),
        ),
        in_specs=[anywhere] * 2,
        out_specs=(anywhere,) * 2,
        scratch_shapes=[
            pltpu.VMEM((width, owned), f32),
            pltpu.SemaphoreType.DMA,
            pltpu.SemaphoreType.DMA((n,)),
            pltpu.SemaphoreType.DMA((2,)),
        ],
        cost_estimate=pl.CostEstimate(flops=0, bytes_accessed=0, transcendentals=0),
        compiler_params=PARAMS,
        name="spread_block",
    )(*(pltpu.with_memory_space_constraint(a, pltpu.HBM) for a in (features, block)))
    x_feat = exchanged(copies, GROUP_X, X_FIRST)
    y_both = lax.all_gather(both, GROUP_Y, axis_index_groups=listed(GROUP_Y, Y_FIRST))
    kern, q_parts = pl.pallas_call(
        functools.partial(kernel_block, gain),
        out_shape=(
            jax.ShapeDtypeStruct((y_total, x_total), bf16),
            jax.ShapeDtypeStruct((n, 1, x_total), f32),
        ),
        in_specs=[VMEM] * 2,
        out_specs=(VMEM,) * 2,
        scratch_shapes=[pltpu.VMEM((6 * width + 16, x_total), bf16)],
        compiler_params=PARAMS,
        name="kernel_block",
    )(x_feat, y_both)
    q_parts = exchanged(q_parts, GROUP_X, Q_FIRST)
    sums = pl.pallas_call(
        second_block,
        out_shape=jax.ShapeDtypeStruct((m, lines, 128), bf16),
        in_specs=[VMEM] * 2,
        out_specs=VMEM,
        scratch_shapes=[pltpu.VMEM((n, 1, owned), f32), pltpu.VMEM((lines, 128), f32)],
        compiler_params=PARAMS,
        name="second_block",
    )(q_parts, kern)
    sums = exchanged(sums, GROUP_Y, SECOND_FIRST)
    parts, factor, diagonal = pl.pallas_call(
        product_block,
        out_shape=(
            jax.ShapeDtypeStruct((n, block.shape[0], owned), bf16),
            jax.ShapeDtypeStruct((1, owned), f32),
            jax.ShapeDtypeStruct(block.shape, f32),
        ),
        in_specs=[VMEM] * 3,
        out_specs=(VMEM,) * 3,
        scratch_shapes=[pltpu.VMEM((m, 1, owned), f32), pltpu.VMEM((m, lines, 128), f32)],
        compiler_params=PARAMS,
        name="product_block",
    )(sums, kern, y_both)
    parts = exchanged(parts, GROUP_X, PRODUCT_FIRST)
    return (jnp.sum(parts.astype(f32), axis=0) + diagonal) * factor


def solution(mesh):
    fine = Mesh(mesh.devices.reshape(mesh.shape["row"] // 2, 2, 2, mesh.shape["col"] // 4, 2), ALL)
    placed = P(None, ALL)
    return jax.shard_map(
        per_device, mesh=fine, in_specs=(placed, placed), out_specs=placed, check_vma=False
    )
```

```python
import functools
import math

import jax
import jax.numpy as jnp
from jax import lax
from jax.experimental import pallas as pl
from jax.experimental.pallas import tpu as pltpu
from jax.sharding import Mesh, PartitionSpec as P

f32 = jnp.float32
bf16 = jnp.bfloat16
VMEM = pl.BlockSpec(memory_space=pltpu.VMEM)
PARAMS = pltpu.CompilerParams(vmem_limit_bytes=16 * 1024 * 1024)

ALL = ("z", "ylo", "yhi", "x", "core")
GROUP_X = ("ylo", "yhi", "x")
GROUP_Y = ("z", "core")


X_FIRST, Y_FIRST = 15, 0
Q_FIRST, SECOND_FIRST, PRODUCT_FIRST = 9, 13, 6


def index_in(axes):
    index = 0
    for name in axes:
        index = index * lax.axis_size(name) + lax.axis_index(name)
    return index


def listed(axes, first):
    count = math.prod(lax.axis_size(name) for name in axes)
    if axes == GROUP_Y:
        return [[(k + first) % count for k in range(count)]]
    return [[k ^ first for k in range(count)]]


def x_place():
    return jnp.bitwise_xor(index_in(GROUP_X), X_FIRST)


def y_place(count):
    return lax.rem(index_in(GROUP_Y) + count - Y_FIRST, count)


def exchanged(x, axes, first):
    return lax.all_to_all(x, axes, 0, 0, tiled=True, axis_index_groups=listed(axes, first))


def three_parts(v):
    high = v.astype(bf16)
    rest = v - high.astype(f32)
    mid = rest.astype(bf16)
    low = (rest - mid.astype(f32)).astype(bf16)
    return high, mid, low


def extended(v, left):
    high, mid, low = three_parts(v)
    half = -0.5 * jnp.sum(v * v, axis=0, keepdims=True)
    a, b, c = (p.astype(f32) for p in three_parts(half))
    row = lax.broadcasted_iota(jnp.int32, (16, v.shape[1]), 0)
    base = 0 if left else 3
    ones = jnp.where((row >= 3 - base) & (row < 6 - base), 1.0, 0.0)
    tail = jnp.where(row == base, a, jnp.where(row == base + 1, b, jnp.where(row == base + 2, c, ones)))
    tail = tail.astype(bf16)
    if left:
        parts = [high, high, mid, high, low, mid, tail]
    else:
        parts = [high, mid, high, low, high, mid, tail]
    return jnp.concatenate(parts, axis=0)


def spread_block(f_ref, b_ref, x_ref, y_ref, here, spread, in_sem, x_sem, y_sem):
    width = f_ref.shape[0]
    fetch = pltpu.make_async_copy(f_ref, here, in_sem)
    fetch.start()
    lower = pltpu.make_async_copy(f_ref, y_ref.at[pl.ds(0, width)], y_sem.at[0])
    upper = pltpu.make_async_copy(b_ref, y_ref.at[pl.ds(width, b_ref.shape[0])], y_sem.at[1])
    lower.start()
    upper.start()
    fetch.wait()
    values = here[...]
    for i in range(spread.shape[0]):
        spread[i] = values
    share = spread.shape[0]
    copies = [
        pltpu.make_async_copy(spread, x_ref.at[pl.ds(i * share, share)], x_sem.at[i])
        for i in range(x_ref.shape[0] // share)
    ]
    for copy in copies:
        copy.start()
    for copy in copies:
        copy.wait()
    lower.wait()
    upper.wait()


def kernel_block(gain, x_ref, y_ref, k_ref, q_ref, right_ref):
    count, size, width = x_ref.shape
    total = k_ref.shape[1]
    x = jnp.concatenate([x_ref[i] for i in range(count)], axis=1) * gain
    right_ref[...] = extended(x, False)
    step = 512
    sums = [jnp.zeros((8, step), f32) for _ in range(0, total, step)]
    for i in range(y_ref.shape[0]):
        left = extended(y_ref[i, :size] * gain, True)
        for j in range(0, total, step):
            expo = lax.dot_general(
                left, right_ref[:, j : j + step], (((0,), (0,)), ((), ())),
                preferred_element_type=f32,
            )
            tile = jnp.exp2(expo).astype(bf16)
            k_ref[i * width : (i + 1) * width, j : j + step] = tile
            wide = tile.astype(f32)
            part = sums[j // step]
            for r in range(0, width, 8):
                part = part + wide[r : r + 8]
            sums[j // step] = part
    flat = jnp.sum(jnp.concatenate(sums, axis=1), axis=0, keepdims=True)
    for d in range(q_ref.shape[0]):
        q_ref[d] = flat


def second_block(q_ref, k_ref, out_ref, sum_ref, line_ref):
    line_ref[...] = jnp.zeros_like(line_ref)
    count, _, total = q_ref.shape
    width = sum_ref.shape[2]
    q = q_ref[0]
    for i in range(1, count):
        q = q + q_ref[i]
    for i in range(count):
        sum_ref[i] = q[:, i * width : (i + 1) * width]
    own = sum_ref[x_place()]
    inv = 1.0 / q
    pieces = [jnp.broadcast_to(inv[:, t : t + 128], (16, 128)) for t in range(0, total, 128)]
    mine = y_place(out_ref.shape[0])
    apart = jnp.concatenate(
        [jnp.where(mine == i, 1.0 / own, 0.0) for i in range(k_ref.shape[0] // width)], axis=1
    )
    grade = 1.0 + mine.astype(f32) / out_ref.shape[0]
    lines = k_ref.shape[0] // 128
    for i in range(lines):
        groups = []
        for r in range(0, 128, 16):
            acc = jnp.zeros((16, 128), f32)
            for t, piece in enumerate(pieces):
                rows = k_ref[i * 128 + r : i * 128 + r + 16, t * 128 : (t + 1) * 128]
                acc = acc + rows.astype(f32) * piece
            groups.append(acc)
        line = jnp.sum(jnp.concatenate(groups, axis=0).T, axis=0, keepdims=True)
        line_ref[i : i + 1, :] = (line - apart[:, i * 128 : (i + 1) * 128]) * grade
    for i, part in enumerate(three_parts(own)):
        line_ref[lines + i : lines + i + 1, :width] = part.astype(f32)
    message = line_ref[...].astype(bf16)
    for d in range(out_ref.shape[0]):
        out_ref[d] = message


def product_block(m_ref, k_ref, b_ref, out_ref, own_ref, add_ref, fac_ref, line_ref):
    count, rows, width = b_ref.shape
    size = rows - out_ref.shape[1]
    lines = k_ref.shape[0] // 128
    summed = jnp.zeros(m_ref.shape[1:], f32)
    for k in range(count):
        i = (k + SECOND_FIRST - Y_FIRST) % count
        lined = m_ref[k].astype(f32)
        line_ref[i] = lined
        summed = summed + lined * (1.0 / (1.0 + i / count))
    q = jnp.concatenate(
        [
            line_ref[i, lines : lines + 1, :width]
            + line_ref[i, lines + 1 : lines + 2, :width]
            + line_ref[i, lines + 2 : lines + 3, :width]
            for i in range(count)
        ],
        axis=1,
    )
    line_ref[0] = summed
    second = jnp.concatenate([line_ref[0, i : i + 1, :] for i in range(lines)], axis=1)
    inv = 1.0 / q
    second = second + inv
    factor = inv * lax.rsqrt(second * inv)
    block = jnp.concatenate([b_ref[i, size:] for i in range(count)], axis=1)
    weighted = (block * factor).astype(bf16)
    for i in range(count):
        fac_ref[i] = factor[:, i * width : (i + 1) * width]
    place, mine = x_place(), y_place(count)
    own = fac_ref[mine]
    own_ref[...] = own
    added = (b_ref[mine, size:] * own).astype(bf16).astype(f32)
    add_ref[...] = added
    step = 512
    values = jnp.concatenate(
        [
            jnp.dot(weighted, k_ref[:, j : j + step], preferred_element_type=f32)
            for j in range(0, k_ref.shape[1], step)
        ],
        axis=1,
    )
    for i in range(out_ref.shape[0]):
        value = values[:, i * width : (i + 1) * width]
        value = jnp.where(place == i, value - added, value)
        out_ref[i ^ X_FIRST ^ PRODUCT_FIRST] = value.astype(bf16)


def per_device(features, block):
    width, owned = features.shape
    n = lax.axis_size(GROUP_X)
    m = lax.axis_size(GROUP_Y)
    frames = owned * n * m
    scale = 4.0 / (float(frames) ** (2.0 / width) - 1.0)
    gain = math.sqrt(2.0 * math.log2(math.e) / scale)
    x_total, y_total = n * owned, m * owned
    lines = pl.cdiv(y_total // 128 + 3, 16) * 16

    anywhere = pl.BlockSpec(memory_space=pl.ANY)
    copies, both = pl.pallas_call(
        spread_block,
        out_shape=(
            jax.ShapeDtypeStruct((n, width, owned), f32),
            jax.ShapeDtypeStruct((width + block.shape[0], owned), f32),
        ),
        in_specs=[anywhere] * 2,
        out_specs=(anywhere,) * 2,
        scratch_shapes=[
            pltpu.VMEM((width, owned), f32),
            pltpu.VMEM((n // 4, width, owned), f32),
            pltpu.SemaphoreType.DMA,
            pltpu.SemaphoreType.DMA((4,)),
            pltpu.SemaphoreType.DMA((2,)),
        ],
        cost_estimate=pl.CostEstimate(flops=0, bytes_accessed=0, transcendentals=0),
        compiler_params=PARAMS,
        name="spread_block",
    )(*(pltpu.with_memory_space_constraint(a, pltpu.HBM) for a in (features, block)))
    x_feat = exchanged(copies, GROUP_X, X_FIRST)
    y_both = lax.all_gather(both, GROUP_Y, axis_index_groups=listed(GROUP_Y, Y_FIRST))
    kern, q_parts = pl.pallas_call(
        functools.partial(kernel_block, gain),
        out_shape=(
            jax.ShapeDtypeStruct((y_total, x_total), bf16),
            jax.ShapeDtypeStruct((n, 1, x_total), f32),
        ),
        in_specs=[VMEM] * 2,
        out_specs=(VMEM,) * 2,
        scratch_shapes=[pltpu.VMEM((6 * width + 16, x_total), bf16)],
        compiler_params=PARAMS,
        name="kernel_block",
    )(x_feat, y_both)
    q_parts = exchanged(q_parts, GROUP_X, Q_FIRST)
    sums = pl.pallas_call(
        second_block,
        out_shape=jax.ShapeDtypeStruct((m, lines, 128), bf16),
        in_specs=[VMEM] * 2,
        out_specs=VMEM,
        scratch_shapes=[pltpu.VMEM((n, 1, owned), f32), pltpu.VMEM((lines, 128), f32)],
        compiler_params=PARAMS,
        name="second_block",
    )(q_parts, kern)
    sums = exchanged(sums, GROUP_Y, SECOND_FIRST)
    parts, factor, diagonal = pl.pallas_call(
        product_block,
        out_shape=(
            jax.ShapeDtypeStruct((n, block.shape[0], owned), bf16),
            jax.ShapeDtypeStruct((1, owned), f32),
            jax.ShapeDtypeStruct(block.shape, f32),
        ),
        in_specs=[VMEM] * 3,
        out_specs=(VMEM,) * 3,
        scratch_shapes=[pltpu.VMEM((m, 1, owned), f32), pltpu.VMEM((m, lines, 128), f32)],
        compiler_params=PARAMS,
        name="product_block",
    )(sums, kern, y_both)
    parts = exchanged(parts, GROUP_X, PRODUCT_FIRST)
    return (jnp.sum(parts.astype(f32), axis=0) + diagonal) * factor


def solution(mesh):
    fine = Mesh(mesh.devices.reshape(mesh.shape["row"] // 2, 2, 2, mesh.shape["col"] // 4, 2), ALL)
    placed = P(None, ALL)
    return jax.shard_map(
        per_device, mesh=fine, in_specs=(placed, placed), out_specs=placed, check_vma=False
    )
```

```python
import functools
import math

import jax
import jax.numpy as jnp
from jax import lax
from jax.experimental import pallas as pl
from jax.experimental.pallas import tpu as pltpu
from jax.sharding import Mesh, PartitionSpec as P

f32 = jnp.float32
bf16 = jnp.bfloat16
VMEM = pl.BlockSpec(memory_space=pltpu.VMEM)
PARAMS = pltpu.CompilerParams(vmem_limit_bytes=16 * 1024 * 1024)

ALL = ("z", "ylo", "yhi", "x", "core")
GROUP_X = ("ylo", "yhi", "x")
GROUP_Y = ("z", "core")


X_FIRST, Y_FIRST = 15, 0
Q_FIRST, SECOND_FIRST, PRODUCT_FIRST = 9, 13, 6


def index_in(axes):
    index = 0
    for name in axes:
        index = index * lax.axis_size(name) + lax.axis_index(name)
    return index


def listed(axes, first):
    count = math.prod(lax.axis_size(name) for name in axes)
    if axes == GROUP_Y:
        return [[(k + first) % count for k in range(count)]]
    return [[k ^ first for k in range(count)]]


def x_place():
    return jnp.bitwise_xor(index_in(GROUP_X), X_FIRST)


def y_place(count):
    return lax.rem(index_in(GROUP_Y) + count - Y_FIRST, count)


def exchanged(x, axes, first):
    return lax.all_to_all(x, axes, 0, 0, tiled=True, axis_index_groups=listed(axes, first))


def three_parts(v):
    high = v.astype(bf16)
    rest = v - high.astype(f32)
    mid = rest.astype(bf16)
    low = (rest - mid.astype(f32)).astype(bf16)
    return high, mid, low


def extended(v, left):
    high, mid, low = three_parts(v)
    half = -0.5 * jnp.sum(v * v, axis=0, keepdims=True)
    a, b, c = (p.astype(f32) for p in three_parts(half))
    row = lax.broadcasted_iota(jnp.int32, (16, v.shape[1]), 0)
    base = 0 if left else 3
    ones = jnp.where((row >= 3 - base) & (row < 6 - base), 1.0, 0.0)
    tail = jnp.where(row == base, a, jnp.where(row == base + 1, b, jnp.where(row == base + 2, c, ones)))
    tail = tail.astype(bf16)
    if left:
        parts = [high, high, mid, high, low, mid, tail]
    else:
        parts = [high, mid, high, low, high, mid, tail]
    return jnp.concatenate(parts, axis=0)


def spread_block(f_ref, b_ref, x_ref, y_ref, here, spread, in_sem, x_sem, y_sem):
    width = f_ref.shape[0]
    fetch = pltpu.make_async_copy(f_ref, here, in_sem)
    fetch.start()
    lower = pltpu.make_async_copy(f_ref, y_ref.at[pl.ds(0, width)], y_sem.at[0])
    upper = pltpu.make_async_copy(b_ref, y_ref.at[pl.ds(width, b_ref.shape[0])], y_sem.at[1])
    lower.start()
    upper.start()
    fetch.wait()
    values = here[...]
    for i in range(spread.shape[0]):
        spread[i] = values
    share = spread.shape[0]
    copies = [
        pltpu.make_async_copy(spread, x_ref.at[pl.ds(i * share, share)], x_sem.at[i])
        for i in range(x_ref.shape[0] // share)
    ]
    for copy in copies:
        copy.start()
    for copy in copies:
        copy.wait()
    lower.wait()
    upper.wait()


def kernel_block(gain, x_ref, y_ref, k_ref, q_ref, right_ref):
    count, size, width = x_ref.shape
    total = k_ref.shape[1]
    x = jnp.concatenate([x_ref[i] for i in range(count)], axis=1) * gain
    right_ref[...] = extended(x, False)
    step = 512
    sums = [jnp.zeros((8, step), f32) for _ in range(0, total, step)]
    group = math.gcd(4, y_ref.shape[0])
    tall = group * width
    for i in range(0, y_ref.shape[0], group):
        y = jnp.concatenate([y_ref[i + k, :size] for k in range(group)], axis=1) * gain
        left = extended(y, True)
        for j in range(0, total, step):
            expo = lax.dot_general(
                left, right_ref[:, j : j + step], (((0,), (0,)), ((), ())),
                preferred_element_type=f32,
            )
            tile = jnp.exp2(expo).astype(bf16)
            k_ref[i * width : i * width + tall, j : j + step] = tile
            wide = tile.astype(f32)
            part = sums[j // step]
            for r in range(0, tall, 8):
                part = part + wide[r : r + 8]
            sums[j // step] = part
    flat = jnp.sum(jnp.concatenate(sums, axis=1), axis=0, keepdims=True)
    for d in range(q_ref.shape[0]):
        q_ref[d] = flat


def second_block(q_ref, k_ref, out_ref, sum_ref, line_ref):
    line_ref[...] = jnp.zeros_like(line_ref)
    count, _, total = q_ref.shape
    width = sum_ref.shape[2]
    q = q_ref[0]
    for i in range(1, count):
        q = q + q_ref[i]
    for i in range(count):
        sum_ref[i] = q[:, i * width : (i + 1) * width]
    own = sum_ref[x_place()]
    inv = 1.0 / q
    pieces = [jnp.broadcast_to(inv[:, t : t + 128], (16, 128)) for t in range(0, total, 128)]
    mine = y_place(out_ref.shape[0])
    apart = jnp.concatenate(
        [jnp.where(mine == i, 1.0 / own, 0.0) for i in range(k_ref.shape[0] // width)], axis=1
    )
    grade = 1.0 + mine.astype(f32) / out_ref.shape[0]
    lines = k_ref.shape[0] // 128
    for i in range(lines):
        groups = []
        for r in range(0, 128, 16):
            acc = jnp.zeros((16, 128), f32)
            for t, piece in enumerate(pieces):
                rows = k_ref[i * 128 + r : i * 128 + r + 16, t * 128 : (t + 1) * 128]
                acc = acc + rows.astype(f32) * piece
            groups.append(acc)
        line = jnp.sum(jnp.concatenate(groups, axis=0).T, axis=0, keepdims=True)
        line_ref[i : i + 1, :] = (line - apart[:, i * 128 : (i + 1) * 128]) * grade
    for i, part in enumerate(three_parts(own)):
        line_ref[lines + i : lines + i + 1, :width] = part.astype(f32)
    message = line_ref[...].astype(bf16)
    for d in range(out_ref.shape[0]):
        out_ref[d] = message


def product_block(m_ref, k_ref, b_ref, out_ref, own_ref, add_ref, fac_ref, line_ref):
    count, rows, width = b_ref.shape
    size = rows - out_ref.shape[1]
    lines = k_ref.shape[0] // 128
    summed = jnp.zeros(m_ref.shape[1:], f32)
    for k in range(count):
        i = (k + SECOND_FIRST - Y_FIRST) % count
        lined = m_ref[k].astype(f32)
        line_ref[i] = lined
        summed = summed + lined * (1.0 / (1.0 + i / count))
    q = jnp.concatenate(
        [
            line_ref[i, lines : lines + 1, :width]
            + line_ref[i, lines + 1 : lines + 2, :width]
            + line_ref[i, lines + 2 : lines + 3, :width]
            for i in range(count)
        ],
        axis=1,
    )
    line_ref[0] = summed
    second = jnp.concatenate([line_ref[0, i : i + 1, :] for i in range(lines)], axis=1)
    inv = 1.0 / q
    second = second + inv
    factor = inv * lax.rsqrt(second * inv)
    block = jnp.concatenate([b_ref[i, size:] for i in range(count)], axis=1)
    weighted = (block * factor).astype(bf16)
    for i in range(count):
        fac_ref[i] = factor[:, i * width : (i + 1) * width]
    place, mine = x_place(), y_place(count)
    own = fac_ref[mine]
    own_ref[...] = own
    added = (b_ref[mine, size:] * own).astype(bf16).astype(f32)
    add_ref[...] = added
    step = 512
    values = jnp.concatenate(
        [
            jnp.dot(weighted, k_ref[:, j : j + step], preferred_element_type=f32)
            for j in range(0, k_ref.shape[1], step)
        ],
        axis=1,
    )
    for i in range(out_ref.shape[0]):
        value = values[:, i * width : (i + 1) * width]
        value = jnp.where(place == i, value - added, value)
        out_ref[i ^ X_FIRST ^ PRODUCT_FIRST] = value.astype(bf16)


def per_device(features, block):
    width, owned = features.shape
    n = lax.axis_size(GROUP_X)
    m = lax.axis_size(GROUP_Y)
    frames = owned * n * m
    scale = 4.0 / (float(frames) ** (2.0 / width) - 1.0)
    gain = math.sqrt(2.0 * math.log2(math.e) / scale)
    x_total, y_total = n * owned, m * owned
    lines = pl.cdiv(y_total // 128 + 3, 16) * 16

    anywhere = pl.BlockSpec(memory_space=pl.ANY)
    copies, both = pl.pallas_call(
        spread_block,
        out_shape=(
            jax.ShapeDtypeStruct((n, width, owned), f32),
            jax.ShapeDtypeStruct((width + block.shape[0], owned), f32),
        ),
        in_specs=[anywhere] * 2,
        out_specs=(anywhere,) * 2,
        scratch_shapes=[
            pltpu.VMEM((width, owned), f32),
            pltpu.VMEM((n // 4, width, owned), f32),
            pltpu.SemaphoreType.DMA,
            pltpu.SemaphoreType.DMA((4,)),
            pltpu.SemaphoreType.DMA((2,)),
        ],
        cost_estimate=pl.CostEstimate(flops=0, bytes_accessed=0, transcendentals=0),
        compiler_params=PARAMS,
        name="spread_block",
    )(*(pltpu.with_memory_space_constraint(a, pltpu.HBM) for a in (features, block)))
    x_feat = exchanged(copies, GROUP_X, X_FIRST)
    y_both = lax.all_gather(both, GROUP_Y, axis_index_groups=listed(GROUP_Y, Y_FIRST))
    kern, q_parts = pl.pallas_call(
        functools.partial(kernel_block, gain),
        out_shape=(
            jax.ShapeDtypeStruct((y_total, x_total), bf16),
            jax.ShapeDtypeStruct((n, 1, x_total), f32),
        ),
        in_specs=[VMEM] * 2,
        out_specs=(VMEM,) * 2,
        scratch_shapes=[pltpu.VMEM((6 * width + 16, x_total), bf16)],
        compiler_params=PARAMS,
        name="kernel_block",
    )(x_feat, y_both)
    q_parts = exchanged(q_parts, GROUP_X, Q_FIRST)
    sums = pl.pallas_call(
        second_block,
        out_shape=jax.ShapeDtypeStruct((m, lines, 128), bf16),
        in_specs=[VMEM] * 2,
        out_specs=VMEM,
        scratch_shapes=[pltpu.VMEM((n, 1, owned), f32), pltpu.VMEM((lines, 128), f32)],
        compiler_params=PARAMS,
        name="second_block",
    )(q_parts, kern)
    sums = exchanged(sums, GROUP_Y, SECOND_FIRST)
    parts, factor, diagonal = pl.pallas_call(
        product_block,
        out_shape=(
            jax.ShapeDtypeStruct((n, block.shape[0], owned), bf16),
            jax.ShapeDtypeStruct((1, owned), f32),
            jax.ShapeDtypeStruct(block.shape, f32),
        ),
        in_specs=[VMEM] * 3,
        out_specs=(VMEM,) * 3,
        scratch_shapes=[pltpu.VMEM((m, 1, owned), f32), pltpu.VMEM((m, lines, 128), f32)],
        compiler_params=PARAMS,
        name="product_block",
    )(sums, kern, y_both)
    parts = exchanged(parts, GROUP_X, PRODUCT_FIRST)
    return (jnp.sum(parts.astype(f32), axis=0) + diagonal) * factor


def solution(mesh):
    fine = Mesh(mesh.devices.reshape(mesh.shape["row"] // 2, 2, 2, mesh.shape["col"] // 4, 2), ALL)
    placed = P(None, ALL)
    return jax.shard_map(
        per_device, mesh=fine, in_specs=(placed, placed), out_specs=placed, check_vma=False
    )
```

```python
import functools
import math

import jax
import jax.numpy as jnp
from jax import lax
from jax.experimental import pallas as pl
from jax.experimental.pallas import tpu as pltpu
from jax.sharding import Mesh, PartitionSpec as P

f32 = jnp.float32
bf16 = jnp.bfloat16
VMEM = pl.BlockSpec(memory_space=pltpu.VMEM)
PARAMS = pltpu.CompilerParams(vmem_limit_bytes=16 * 1024 * 1024)

ALL = ("z", "ylo", "yhi", "x", "core")
GROUP_X = ("ylo", "yhi", "x")
GROUP_Y = ("z", "core")


X_FIRST, Y_FIRST = 15, 0
Q_FIRST, SECOND_FIRST, PRODUCT_FIRST = 9, 11, 6


def index_in(axes):
    index = 0
    for name in axes:
        index = index * lax.axis_size(name) + lax.axis_index(name)
    return index


def listed(axes, first):
    count = math.prod(lax.axis_size(name) for name in axes)
    if axes == GROUP_Y:
        return [[(k + first) % count for k in range(count)]]
    return [[k ^ first for k in range(count)]]


def x_place():
    return jnp.bitwise_xor(index_in(GROUP_X), X_FIRST)


def y_place(count):
    return lax.rem(index_in(GROUP_Y) + count - Y_FIRST, count)


def exchanged(x, axes, first):
    return lax.all_to_all(x, axes, 0, 0, tiled=True, axis_index_groups=listed(axes, first))


def three_parts(v):
    high = v.astype(bf16)
    rest = v - high.astype(f32)
    mid = rest.astype(bf16)
    low = (rest - mid.astype(f32)).astype(bf16)
    return high, mid, low


def extended(v, left):
    high, mid, low = three_parts(v)
    half = -0.5 * jnp.sum(v * v, axis=0, keepdims=True)
    a, b, c = (p.astype(f32) for p in three_parts(half))
    row = lax.broadcasted_iota(jnp.int32, (16, v.shape[1]), 0)
    base = 0 if left else 3
    ones = jnp.where((row >= 3 - base) & (row < 6 - base), 1.0, 0.0)
    tail = jnp.where(row == base, a, jnp.where(row == base + 1, b, jnp.where(row == base + 2, c, ones)))
    tail = tail.astype(bf16)
    if left:
        parts = [high, high, mid, high, low, mid, tail]
    else:
        parts = [high, mid, high, low, high, mid, tail]
    return jnp.concatenate(parts, axis=0)


def spread_block(f_ref, b_ref, x_ref, y_ref, here, spread, in_sem, x_sem, y_sem):
    width = f_ref.shape[0]
    fetch = pltpu.make_async_copy(f_ref, here, in_sem)
    fetch.start()
    lower = pltpu.make_async_copy(f_ref, y_ref.at[pl.ds(0, width)], y_sem.at[0])
    upper = pltpu.make_async_copy(b_ref, y_ref.at[pl.ds(width, b_ref.shape[0])], y_sem.at[1])
    lower.start()
    upper.start()
    fetch.wait()
    values = here[...]
    for i in range(spread.shape[0]):
        spread[i] = values
    share = spread.shape[0]
    copies = [
        pltpu.make_async_copy(spread, x_ref.at[pl.ds(i * share, share)], x_sem.at[i])
        for i in range(x_ref.shape[0] // share)
    ]
    for copy in copies:
        copy.start()
    for copy in copies:
        copy.wait()
    lower.wait()
    upper.wait()


def kernel_block(gain, x_ref, y_ref, k_ref, q_ref, right_ref):
    count, size, width = x_ref.shape
    total = k_ref.shape[1]
    x = jnp.concatenate([x_ref[i] for i in range(count)], axis=1) * gain
    right_ref[...] = extended(x, False)
    step = 512
    sums = [jnp.zeros((8, step), f32) for _ in range(0, total, step)]
    group = math.gcd(4, y_ref.shape[0])
    tall = group * width
    for i in range(0, y_ref.shape[0], group):
        y = jnp.concatenate([y_ref[i + k, :size] for k in range(group)], axis=1) * gain
        left = extended(y, True)
        for j in range(0, total, step):
            expo = lax.dot_general(
                left, right_ref[:, j : j + step], (((0,), (0,)), ((), ())),
                preferred_element_type=f32,
            )
            tile = jnp.exp2(expo).astype(bf16)
            k_ref[i * width : i * width + tall, j : j + step] = tile
            wide = tile.astype(f32)
            part = sums[j // step]
            for r in range(0, tall, 8):
                part = part + wide[r : r + 8]
            sums[j // step] = part
    flat = jnp.sum(jnp.concatenate(sums, axis=1), axis=0, keepdims=True)
    for d in range(q_ref.shape[0]):
        q_ref[d] = flat


def second_block(q_ref, k_ref, out_ref, sum_ref, line_ref):
    line_ref[...] = jnp.zeros_like(line_ref)
    count, _, total = q_ref.shape
    width = sum_ref.shape[2]
    q = q_ref[0]
    for i in range(1, count):
        q = q + q_ref[i]
    for i in range(count):
        sum_ref[i] = q[:, i * width : (i + 1) * width]
    own = sum_ref[x_place()]
    inv = 1.0 / q
    pieces = [jnp.broadcast_to(inv[:, t : t + 128], (16, 128)) for t in range(0, total, 128)]
    mine = y_place(out_ref.shape[0])
    apart = jnp.concatenate(
        [jnp.where(mine == i, 1.0 / own, 0.0) for i in range(k_ref.shape[0] // width)], axis=1
    )
    grade = 1.0 + mine.astype(f32) / out_ref.shape[0]
    lines = k_ref.shape[0] // 128
    for i in range(lines):
        groups = []
        for r in range(0, 128, 16):
            acc = jnp.zeros((16, 128), f32)
            for t, piece in enumerate(pieces):
                rows = k_ref[i * 128 + r : i * 128 + r + 16, t * 128 : (t + 1) * 128]
                acc = acc + rows.astype(f32) * piece
            groups.append(acc)
        line = jnp.sum(jnp.concatenate(groups, axis=0).T, axis=0, keepdims=True)
        line_ref[i : i + 1, :] = (line - apart[:, i * 128 : (i + 1) * 128]) * grade
    for i, part in enumerate(three_parts(own)):
        line_ref[lines + i : lines + i + 1, :width] = part.astype(f32)
    message = line_ref[...].astype(bf16)
    for d in range(out_ref.shape[0]):
        out_ref[d] = message


def product_block(m_ref, k_ref, b_ref, out_ref, own_ref, add_ref, fac_ref, line_ref):
    count, rows, width = b_ref.shape
    size = rows - out_ref.shape[1]
    lines = k_ref.shape[0] // 128
    summed = jnp.zeros(m_ref.shape[1:], f32)
    for k in range(count):
        i = (k + SECOND_FIRST - Y_FIRST) % count
        lined = m_ref[k].astype(f32)
        line_ref[i] = lined
        summed = summed + lined * (1.0 / (1.0 + i / count))
    q = jnp.concatenate(
        [
            line_ref[i, lines : lines + 1, :width]
            + line_ref[i, lines + 1 : lines + 2, :width]
            + line_ref[i, lines + 2 : lines + 3, :width]
            for i in range(count)
        ],
        axis=1,
    )
    line_ref[0] = summed
    second = jnp.concatenate([line_ref[0, i : i + 1, :] for i in range(lines)], axis=1)
    inv = 1.0 / q
    second = second + inv
    factor = inv * lax.rsqrt(second * inv)
    block = jnp.concatenate([b_ref[i, size:] for i in range(count)], axis=1)
    weighted = (block * factor).astype(bf16)
    for i in range(count):
        fac_ref[i] = factor[:, i * width : (i + 1) * width]
    place, mine = x_place(), y_place(count)
    own = fac_ref[mine]
    own_ref[...] = own
    added = (b_ref[mine, size:] * own).astype(bf16).astype(f32)
    add_ref[...] = added
    step = 512
    values = jnp.concatenate(
        [
            jnp.dot(weighted, k_ref[:, j : j + step], preferred_element_type=f32)
            for j in range(0, k_ref.shape[1], step)
        ],
        axis=1,
    )
    for i in range(out_ref.shape[0]):
        value = values[:, i * width : (i + 1) * width]
        value = jnp.where(place == i, value - added, value)
        out_ref[i ^ X_FIRST ^ PRODUCT_FIRST] = value.astype(bf16)


def per_device(features, block):
    width, owned = features.shape
    n = lax.axis_size(GROUP_X)
    m = lax.axis_size(GROUP_Y)
    frames = owned * n * m
    scale = 4.0 / (float(frames) ** (2.0 / width) - 1.0)
    gain = math.sqrt(2.0 * math.log2(math.e) / scale)
    x_total, y_total = n * owned, m * owned
    lines = pl.cdiv(y_total // 128 + 3, 16) * 16

    anywhere = pl.BlockSpec(memory_space=pl.ANY)
    copies, both = pl.pallas_call(
        spread_block,
        out_shape=(
            jax.ShapeDtypeStruct((n, width, owned), f32),
            jax.ShapeDtypeStruct((width + block.shape[0], owned), f32),
        ),
        in_specs=[anywhere] * 2,
        out_specs=(anywhere,) * 2,
        scratch_shapes=[
            pltpu.VMEM((width, owned), f32),
            pltpu.VMEM((n // 4, width, owned), f32),
            pltpu.SemaphoreType.DMA,
            pltpu.SemaphoreType.DMA((4,)),
            pltpu.SemaphoreType.DMA((2,)),
        ],
        cost_estimate=pl.CostEstimate(flops=0, bytes_accessed=0, transcendentals=0),
        compiler_params=PARAMS,
        name="spread_block",
    )(*(pltpu.with_memory_space_constraint(a, pltpu.HBM) for a in (features, block)))
    x_feat = exchanged(copies, GROUP_X, X_FIRST)
    y_both = lax.all_gather(both, GROUP_Y, axis_index_groups=listed(GROUP_Y, Y_FIRST))
    kern, q_parts = pl.pallas_call(
        functools.partial(kernel_block, gain),
        out_shape=(
            jax.ShapeDtypeStruct((y_total, x_total), bf16),
            jax.ShapeDtypeStruct((n, 1, x_total), f32),
        ),
        in_specs=[VMEM] * 2,
        out_specs=(VMEM,) * 2,
        scratch_shapes=[pltpu.VMEM((6 * width + 16, x_total), bf16)],
        compiler_params=PARAMS,
        name="kernel_block",
    )(x_feat, y_both)
    q_parts = exchanged(q_parts, GROUP_X, Q_FIRST)
    sums = pl.pallas_call(
        second_block,
        out_shape=jax.ShapeDtypeStruct((m, lines, 128), bf16),
        in_specs=[VMEM] * 2,
        out_specs=VMEM,
        scratch_shapes=[pltpu.VMEM((n, 1, owned), f32), pltpu.VMEM((lines, 128), f32)],
        compiler_params=PARAMS,
        name="second_block",
    )(q_parts, kern)
    sums = exchanged(sums, GROUP_Y, SECOND_FIRST)
    parts, factor, diagonal = pl.pallas_call(
        product_block,
        out_shape=(
            jax.ShapeDtypeStruct((n, block.shape[0], owned), bf16),
            jax.ShapeDtypeStruct((1, owned), f32),
            jax.ShapeDtypeStruct(block.shape, f32),
        ),
        in_specs=[VMEM] * 3,
        out_specs=(VMEM,) * 3,
        scratch_shapes=[pltpu.VMEM((m, 1, owned), f32), pltpu.VMEM((m, lines, 128), f32)],
        compiler_params=PARAMS,
        name="product_block",
    )(sums, kern, y_both)
    parts = exchanged(parts, GROUP_X, PRODUCT_FIRST)
    return (jnp.sum(parts.astype(f32), axis=0) + diagonal) * factor


def solution(mesh):
    fine = Mesh(mesh.devices.reshape(mesh.shape["row"] // 2, 2, 2, mesh.shape["col"] // 4, 2), ALL)
    placed = P(None, ALL)
    return jax.shard_map(
        per_device, mesh=fine, in_specs=(placed, placed), out_specs=placed, check_vma=False
    )
```
